256 devices in a mesh: dp: 16 (over x, z_hi, core), tensor: 16 (over y, z_lo).
Axes of the slice: x: 4, y: 4, z: 8 (z_hi: 2, z_lo: 4; z = z_hi * 4 + z_lo), core: 2. Of those that a mesh axis runs over, the one named last changes fastest.
Arguments:
- attn_out: bfloat16 [2048, 16384], P('dp', 'tensor'), may hold values from -6 to 6
- teacher_resid: bfloat16 [2048, 16384], P('tensor', 'dp'), may hold values from -6 to 6
- w_out: bfloat16 [16384, 16384], P('tensor', 'dp'), may hold values from -0.046875 to 0.046875
- projection: bfloat16 [16384, 4096], P('dp', 'tensor'), may hold values from -0.046875 to 0.046875
- student_in: bfloat16 [2048, 4096], P('dp', 'tensor'), may hold values from -6 to 6
- gate_act: bfloat16 [2048, 14336], P('dp', 'tensor'), may hold values from -6 to 6
- up_act: bfloat16 [2048, 14336], P('dp', 'tensor'), may hold values from -6 to 6
- w_down: bfloat16 [14336, 4096], P('tensor'), may hold values from -0.046875 to 0.046875
Outputs:
- gate_grad: float32 [2048, 14336], P('dp', 'tensor')
- up_grad: float32 [2048, 14336], P('dp', 'tensor')
- down_grad: float32 [14336, 4096], P('tensor', 'dp')
The draws below stay inside these ranges and needn't reach their ends.
All inputs are finite; a program needn't handle non-finite values.
Results may differ from the reference program's by a relative error of at most 0.029.
Values may be sent and summed in bfloat16 or wider, within the bound.
A program may use at most 128 MiB of HBM per device.

```python
import jax
import jax.numpy as jnp
from jax import lax

DT = 16384
DS = 4096
FFS = 14336
TOK_DEV = 128
TOKENS = 2048
N_DP = 16


def steps_of(stream_key, extent, shards, smallest, high):
    level = 1.0
    for position, parts in shards:
        draws = jax.random.uniform(jax.random.fold_in(jax.random.fold_in(stream_key, 6), position), (parts,), jnp.float32, smallest / len(shards), high / len(shards))
        level = level * jnp.repeat(jnp.exp(draws), extent[position] // parts).reshape((-1,) + (1,) * (len(extent) - 1 - position))
    return level


def centred(stream_key, extent, width, most, shards=(), dtype=jnp.bfloat16):
    factor_of = steps_of(stream_key, extent, shards, -0.22, 0.18) if shards else 1.0
    values = jax.random.normal(stream_key, extent, jnp.float32) * width * factor_of
    return jnp.minimum(jnp.maximum(values, -most), most).astype(dtype)


def setup_inputs(seed: int = 0) -> dict:
    splits = jax.random.split(jax.random.key(seed), 9)
    attn_out = centred(splits[0], (TOKENS, DT), 1.0, 6.0, ((0, 16), (1, 16)))
    teacher_resid = centred(splits[1], (TOKENS, DT), 1.0, 6.0, ((0, 16), (1, 16)))
    w_out = centred(splits[2], (DT, DT), DT ** -0.5, 0.046875, ((0, 16), (1, 16)))
    projection = centred(splits[3], (DT, DS), DT ** -0.5, 0.046875, ((0, 16), (1, 16)))
    student_in = centred(splits[4], (TOKENS, DS), 1.0, 6.0, ((0, 16), (1, 16)))
    gate_act = centred(splits[5], (TOKENS, FFS), 1.0, 6.0, ((0, 16), (1, 16)))
    up_act = centred(splits[6], (TOKENS, FFS), 1.0, 6.0, ((0, 16), (1, 16)))
    w_down = centred(splits[7], (FFS, DS), FFS ** -0.5, 0.046875, ((0, 16),))
    return {"attn_out": attn_out, "teacher_resid": teacher_resid, "w_out": w_out, "projection": projection, "student_in": student_in, "gate_act": gate_act, "up_act": up_act, "w_down": w_down}


def reference(attn_out, teacher_resid, w_out, projection, student_in, gate_act, up_act, w_down):
    mixed_heads = jnp.dot(attn_out, w_out, preferred_element_type=jnp.float32)
    teacher_state = (teacher_resid.astype(jnp.float32) + mixed_heads).astype(jnp.bfloat16)
    target = jnp.dot(teacher_state, projection, preferred_element_type=jnp.float32)
    gate_f = gate_act.astype(jnp.float32)
    up_f = up_act.astype(jnp.float32)
    sigmoid_gate = jax.nn.sigmoid(gate_f)
    hidden = (gate_f * sigmoid_gate * up_f).astype(jnp.bfloat16)
    student_out = student_in.astype(jnp.float32) + jnp.dot(hidden, w_down, preferred_element_type=jnp.float32)
    mismatch = (student_out - target).astype(jnp.bfloat16)
    hidden_grad = lax.dot_general(mismatch, w_down, (((1,), (1,)), ((), ())), preferred_element_type=jnp.float32)
    gate_grad = hidden_grad * up_f * sigmoid_gate * (1.0 + gate_f * (1.0 - sigmoid_gate))
    up_grad = hidden_grad * gate_f * sigmoid_gate
    grouped_hidden = hidden.reshape(N_DP, TOK_DEV, FFS)
    grouped_mismatch = mismatch.reshape(N_DP, TOK_DEV, DS)

    def add_group(total, pair):
        partial_grad = lax.dot_general(pair[0], pair[1], (((0,), (0,)), ((), ())), preferred_element_type=jnp.float32)
        rounded = lax.optimization_barrier(partial_grad.astype(jnp.bfloat16))
        return total + rounded.astype(jnp.float32), None

    down_grad, _ = lax.scan(add_group, jnp.zeros((FFS, DS), jnp.float32), (grouped_hidden, grouped_mismatch))
    return gate_grad, up_grad, down_grad
```

```python
import functools

import jax
import jax.numpy as jnp
from jax import lax
from jax.experimental import pallas as pl
from jax.experimental.pallas import tpu as pltpu
from jax.sharding import PartitionSpec as P

MESH = pl.DeviceIdType.MESH
F32 = jnp.float32
BF16 = jnp.bfloat16

Q = 2
TOK = 128
S = TOK // Q
DK = 1024
DC = 256
DS = 4096
FF = 896
SKEW = 3

A_SLOTS, B_SLOTS, C_SLOTS, D_SLOTS, E_SLOTS = 12, 9, 7, 5, 15
A0 = 0
B0 = A0 + A_SLOTS * Q
C0 = B0 + B_SLOTS * Q
D0 = C0 + C_SLOTS * Q
E0 = D0 + D_SLOTS * Q
SB0 = E0 + E_SLOTS * Q
H0 = SB0 + B_SLOTS
N_SLOTS = H0 + A_SLOTS


def kernel(
    attn, resid, w_out, proj, stud, gate, up, w_down,
    gate_grad, up_grad, down_grad,
    g, p1, y1, y2, r, zr, ta, p2, ds1, p3, dx, p4, p4b, dz,
    ma, mt, mb, hid, ht, sp, sy1, sy2, sr, szr, so,
    vw_out, vproj, vw_down, vresid, vstud, vgate, vup,
    ss, rs, ls,
):
    d = lax.axis_index("dp")
    t = lax.axis_index("tensor")
    x, zh, c = d // 4, lax.rem(d // 2, 2), lax.rem(d, 2)
    y, zl = t // 4, lax.rem(t, 4)

    def dev(x_, zh_, c_, y_, zl_):
        return ((x_ * 2 + zh_) * 2 + c_, y_ * 4 + zl_)

    def ring(a, k):
        return lax.rem(a + k, 4)

    sib = dev(x, zh, 1 - c, y, zl)
    far = dev(x, 1 - zh, c, y, zl)
    xs = [dev(ring(x, k), zh, c, y, zl) for k in (1, 2, 3)]
    zs = [dev(x, zh, c, y, ring(zl, k)) for k in (1, 2, 3)]
    yn, yp = dev(x, zh, c, ring(y, 1), zl), dev(x, zh, c, ring(y, 3), zl)
    mirror = (t, d)

    def load(i, src, dst):
        return pltpu.make_async_copy(src, dst, ls.at[i])

    own_a = [load(q, attn.at[pl.ds(q * S, S)], g.at[q, x, zh, c]) for q in range(Q)]
    l_gate = load(Q, gate, vgate)
    l_up = load(Q + 1, up, vup)
    l_down = load(Q + 2, w_down, vw_down)
    l_out = load(Q + 3, w_out, vw_out)
    l_proj = load(Q + 4, proj, vproj)
    l_resid = load(Q + 5, resid, vresid)
    l_stud = load(Q + 6, stud, vstud)
    for cp in own_a + [l_gate, l_up, l_down, l_out, l_proj, l_resid, l_stud]:
        cp.start()

    barrier = pltpu.get_barrier_semaphore()
    for peer in [sib, far, yn, yp] + xs + zs:
        pl.semaphore_signal(barrier, 1, device_id=peer, device_id_type=MESH)

    @pl.when(d != t)
    def _():
        pl.semaphore_signal(barrier, 1, device_id=mirror, device_id_type=MESH)

    pl.semaphore_wait(barrier, jnp.where(d != t, 11, 10))

    started = []

    def send(slot, src, dst, peer):
        cp = pltpu.make_async_remote_copy(
            src, dst, ss.at[slot], rs.at[slot], device_id=peer, device_id_type=MESH
        )
        cp.start()
        started.append(cp)
        return cp

    def gather_dp_own(base, own, place, place2):
        dst = place(x, zh, c)
        m = {}
        m["z"] = send(base, own, dst, far)
        for k in (1, 2, 3):
            m["x", k] = send(base + k, own, dst, xs[k - 1])
        m["s0"] = send(base + 4, own, dst, sib)
        return m

    def gather_dp_far(base, m, place, place2):
        m["z"].wait_recv()
        piece = place(x, 1 - zh, c)
        for k in (1, 2, 3):
            m["zx", k] = send(base + 4 + k, piece, piece, xs[k - 1])
        m["s1"] = send(base + 8, piece, piece, sib)

    def gather_dp_sib(base, m, place, place2):
        for k in (1, 3, 2):
            m["x", k].wait_recv()
            m["zx", k].wait_recv()
            piece = place2(ring(x, 4 - k), c)
            m["s", k] = send(base + 8 + k, piece, piece, sib)

    def gather_dp_end(m):
        m["s0"].wait_recv()
        m["s1"].wait_recv()
        for k in (1, 3, 2):
            m["s", k].wait_recv()

    def scatter_y_first(base, part, a1):
        far_y = ring(y, 2)
        m = {}
        m["h0"] = send(base, part.at[far_y, pl.ds(0, 2)], a1.at[0], yn)
        m["h1"] = send(base + 1, part.at[far_y, pl.ds(2, 2)], a1.at[1], yp)
        return m

    def scatter_y_raw(base, m, part, a2):
        m["r0"] = send(base + 2, part.at[ring(y, 1), pl.ds(2, 2)], a2.at[0, pl.ds(2, 2)], yn)
        m["r1"] = send(base + 3, part.at[ring(y, 3), pl.ds(0, 2)], a2.at[1, pl.ds(0, 2)], yp)

    def scatter_y_forward(base, m, part, a1, a2):
        for side, (lo, to, peer) in enumerate(((0, ring(y, 1), yn), (2, ring(y, 3), yp))):
            m["h%d" % side].wait_recv()
            for i in range(2):
                both = part[to, lo + i].astype(F32) + a1[side, i].astype(F32)
                part[to, lo + i] = both.astype(BF16)
            m["c%d" % side] = send(
                base + 4 + side, part.at[to, pl.ds(lo, 2)], a2.at[side, pl.ds(lo, 2)], peer
            )

    def scatter_z(base, m, part, a2, res, az):
        for n in ("r0", "r1", "c0", "c1"):
            m[n].wait_recv()
        for i in range(4):
            total = part[y, i].astype(F32) + a2[0, i].astype(F32) + a2[1, i].astype(F32)
            res[i] = total.astype(BF16)
        for k in (1, 2, 3):
            m["z", k] = send(base + 5 + k, res.at[ring(zl, k)], az.at[k - 1], zs[k - 1])

    def scatter_end(m, res, az):
        for k in (1, 2, 3):
            m["z", k].wait_recv()
        total = res[zl].astype(F32)
        for k in range(3):
            total += az[k].astype(F32)
        return total

    def gather_z(base, view):
        own = view(y, zl, 1)
        return {("z", k): send(base + k - 1, own, own, zs[k - 1]) for k in (1, 2, 3)}

    def gather_y(base, m, view):
        for k in (1, 2, 3):
            m["z", k].wait_recv()
        mine = view(y, 0, 4)
        m["y0"] = send(base + 3, mine, mine, yn)
        m["y1"] = send(base + 4, mine, mine, yp)

    def gather_forward(base, m, view):
        m["y0"].wait_recv()
        half = view(ring(y, 3), 0, 2)
        m["f0"] = send(base + 5, half, half, yn)
        m["y1"].wait_recv()
        half = view(ring(y, 1), 2, 2)
        m["f1"] = send(base + 6, half, half, yp)

    def gather_end(m):
        m["f0"].wait_recv()
        m["f1"].wait_recv()

    A = [None] * Q
    B = [None] * Q
    C = [None] * Q
    D = [{} for _ in range(Q)]
    E = [None] * Q
    EM = [None] * Q

    def g_place(q):
        return lambda x_, zh_, c_: g.at[q, x_, zh_, c_]

    def g_place2(q):
        return lambda x_, c_: g.at[q, x_, :, c_]

    def ta_view(q):
        return lambda y_, lo, n: ta.at[q, y_, pl.ds(lo, n)]

    def ma_view(q):
        def view(y_, lo, n):
            start = pl.multiple_of((y_ * 4 + lo) * DC, DC)
            return ma.at[q, :, pl.ds(start, n * DC)]

        return view

    def mb_view(q):
        rows = pl.ds(q * S, S)

        def view(y_, lo, n):
            if n == 1:
                return mb.at[lax.rem(lo, 2), y_ * 2 + lo // 2, rows]
            if n == 2:
                return mb.at[:, y_ * 2 + lo // 2, rows]
            return mb.at[:, pl.ds(y_ * 2, 2), rows]

        return view

    def mix(q, xg):
        lhs = g[q, xg].reshape(4 * S, DK)

        def cols(n, _):
            at = pl.ds(pl.multiple_of(n * 256, 256), 256)
            out = jnp.dot(lhs, vw_out[:, at], preferred_element_type=F32)
            p1[q, xg, :, :, at] = out.astype(BF16).reshape(4, S, 256)
            return 0

        lax.fori_loop(0, DK // 256, cols, 0)

    def map_target(q, yg):
        out = jnp.dot(ta[q, yg].reshape(4 * S, DK), vproj[...], preferred_element_type=F32)
        p2[q, yg] = out.astype(BF16).reshape(2, 2, S, DC)

    def s_far(q):
        gather_dp_far(A0 + A_SLOTS * q, A[q], g_place(q), g_place2(q))

    def s_sib(q):
        gather_dp_sib(A0 + A_SLOTS * q, A[q], g_place(q), g_place2(q))

    def s_mix(q):
        own_a[q].wait()
        gather_dp_end(A[q])
        base = B0 + B_SLOTS * q
        mix(q, ring(y, 2))
        B[q] = scatter_y_first(base, p1.at[q], y1.at[q])
        mix(q, ring(y, 1))
        mix(q, ring(y, 3))
        scatter_y_raw(base, B[q], p1.at[q], y2.at[q])
        mix(q, y)

    def s_forward(q):
        scatter_y_forward(B0 + B_SLOTS * q, B[q], p1.at[q], y1.at[q], y2.at[q])

    def s_z(q):
        scatter_z(B0 + B_SLOTS * q, B[q], p1.at[q], y2.at[q], r.at[q], zr.at[q])

    def s_state(q):
        total = scatter_end(B[q], r.at[q], zr.at[q])
        state = total + vresid[pl.ds(q * S, S)].astype(F32)
        ta[q, y, zl] = state.astype(BF16)
        C[q] = gather_z(C0 + C_SLOTS * q, ta_view(q))

    def s_all_y(q):
        gather_y(C0 + C_SLOTS * q, C[q], ta_view(q))

    def s_all_forward(q):
        gather_forward(C0 + C_SLOTS * q, C[q], ta_view(q))
        map_target(q, y)
        map_target(q, ring(y, 1))
        map_target(q, ring(y, 3))

    def s_target(q):
        gather_end(C[q])
        map_target(q, ring(y, 2))
        D[q]["s"] = send(D0 + D_SLOTS * q, p2.at[q, :, :, 1 - c], ds1.at[q], sib)

    def s_target_x(q):
        D[q]["s"].wait_recv()
        for i in range(4):
            for j in range(2):
                p3[q, i, j] = (p2[q, i, j, c].astype(F32) + ds1[q, i, j].astype(F32)).astype(BF16)
        for k in (1, 2, 3):
            D[q]["x", k] = send(D0 + D_SLOTS * q + k, p3.at[q, ring(x, k)], dx.at[q, k - 1], xs[k - 1])

    def s_target_z(q):
        for k in (1, 2, 3):
            D[q]["x", k].wait_recv()
        total = p3[q, x].astype(F32)
        for k in range(3):
            total += dx[q, k].astype(F32)
        p4[q] = total
        p4b[q] = total.astype(BF16)
        D[q]["z"] = send(D0 + D_SLOTS * q + 4, p4b.at[q, 1 - zh], dz.at[q], far)

    def s_mismatch(q):
        D[q]["z"].wait_recv()
        rows = pl.ds(q * S, S)
        target = p4[q, zh] + dz[q].astype(F32)
        diff = (vstud[rows].astype(F32) + so[rows] - target).astype(BF16)
        mt[q] = diff
        col = pl.multiple_of(t * DC, DC)
        ma[q, :, pl.ds(col, DC)] = diff
        base = E0 + E_SLOTS * q
        cp = pltpu.make_async_remote_copy(
            mt.at[q], mb_view(q)(y, zl, 1), ss.at[base + 14], rs.at[base + 14],
            device_id=mirror, device_id_type=MESH,
        )

        @pl.when(d != t)
        def _():
            pltpu.make_async_remote_copy(
                mt.at[q], mb.at[lax.rem(d, 2), d // 2, rows], ss.at[base + 14], rs.at[base + 14],
                device_id=mirror, device_id_type=MESH,
            ).start()

        @pl.when(d == t)
        def _():
            mb[lax.rem(d, 2), d // 2, rows] = diff

        EM[q] = cp
        E[q] = gather_z(base, ma_view(q))

    def s_mirror(q):
        @pl.when(d != t)
        def _():
            EM[q].wait()

        base = E0 + E_SLOTS * q + 7
        EM[q] = gather_z(base, mb_view(q))

    def s_mis_y(q):
        gather_y(E0 + E_SLOTS * q, E[q], ma_view(q))
        gather_y(E0 + E_SLOTS * q + 7, EM[q], mb_view(q))

    def s_mis_forward(q):
        gather_forward(E0 + E_SLOTS * q, E[q], ma_view(q))
        gather_forward(E0 + E_SLOTS * q + 7, EM[q], mb_view(q))

    def s_mis_end(q):
        gather_end(E[q])
        gather_end(EM[q])

    st = {}

    def ht_place(x_, zh_, c_):
        return ht.at[c_, :, pl.ds(pl.multiple_of((x_ * 2 + zh_) * TOK, TOK), TOK)]

    def ht_place2(x_, c_):
        return ht.at[c_, :, pl.ds(pl.multiple_of(x_ * 2 * TOK, 2 * TOK), 2 * TOK)]

    def student():
        l_gate.wait()
        l_up.wait()
        gf = vgate[...].astype(F32)
        h = (gf * jax.nn.sigmoid(gf) * vup[...].astype(F32)).astype(BF16)
        hid[...] = h
        l_down.wait()

        def cols(i, _):
            at = pl.ds(pl.multiple_of(i * DC, DC), DC)
            out = jnp.dot(hid[...], vw_down[:, at], preferred_element_type=F32)
            sp[i // 4, lax.rem(i, 4)] = out.astype(BF16)
            return 0

        lax.fori_loop(0, DS // DC, cols, 0)
        st["m"] = scatter_y_first(SB0, sp, sy1)
        scatter_y_raw(SB0, st["m"], sp, sy2)
        ht[c, :, pl.ds(pl.multiple_of((x * 2 + zh) * TOK, TOK), TOK)] = h.astype(F32).T.astype(BF16)

    def student_forward():
        scatter_y_forward(SB0, st["m"], sp, sy1, sy2)

    def student_z():
        scatter_z(SB0, st["m"], sp, sy2, sr, szr)

    def student_end():
        so[...] = scatter_end(st["m"], sr, szr)

    def hidden_own():
        st["h"] = gather_dp_own(H0, ht_place(x, zh, c), ht_place, ht_place2)

    def hidden_far():
        gather_dp_far(H0, st["h"], ht_place, ht_place2)

    def hidden_sib():
        gather_dp_sib(H0, st["h"], ht_place, ht_place2)

    for q in range(Q):
        A[q] = gather_dp_own(A0 + A_SLOTS * q, attn.at[pl.ds(q * S, S)], g_place(q), g_place2(q))
    student()
    for q in range(Q):
        s_far(q)
    student_forward()
    s_sib(0)
    l_out.wait()
    student_z()

    stages = [
        s_mix, s_forward, s_z, s_state, s_all_y, s_all_forward, s_target, s_target_x, s_target_z,
        s_mismatch, s_mirror, s_mis_y, s_mis_forward, s_mis_end,
    ]
    sib_done = 1
    for tick in range(len(stages) + SKEW * (Q - 1)):
        for q in reversed(range(Q)):
            i = tick - SKEW * q
            if 0 <= i < len(stages):
                if stages[i] is s_mismatch and q == 0:
                    l_stud.wait()
                if stages[i] is s_all_forward and q == 0:
                    l_proj.wait()
                if stages[i] is s_state and q == 0:
                    l_resid.wait()
                stages[i](q)
        if tick < Q - 1:
            s_sib(sib_done)
            sib_done += 1
        if tick == max(1, Q - 1):
            hidden_own()
        if tick == max(1, Q - 1) + 1:
            student_end()
            hidden_far()
        if tick == max(1, Q - 1) + 4:
            hidden_sib()

    def grads(i, _):
        at = pl.ds(pl.multiple_of(i * 128, 128), 128)
        weights = vw_down[at, :]
        for q in range(Q):
            rows = pl.ds(q * S, S)
            hg = lax.dot_general(
                ma[q], weights, (((1,), (1,)), ((), ())), preferred_element_type=F32
            )
            gf = vgate[rows, at].astype(F32)
            uf = vup[rows, at].astype(F32)
            sg = jax.nn.sigmoid(gf)
            gate_grad[rows, at] = hg * uf * sg * (1.0 + gf * (1.0 - sg))
            up_grad[rows, at] = hg * gf * sg
        return 0

    lax.fori_loop(0, FF // 128, grads, 0)
    gather_dp_end(st["h"])

    def down(i, _):
        at = pl.ds(pl.multiple_of(i * 128, 128), 128)
        out = jnp.dot(ht[0, at], mb[0].reshape(8 * TOK, DC), preferred_element_type=F32)
        out += jnp.dot(ht[1, at], mb[1].reshape(8 * TOK, DC), preferred_element_type=F32)
        down_grad[at] = out
        return 0

    lax.fori_loop(0, FF // 128, down, 0)
    for cp in started:
        cp.wait_send()


def per_device(attn_out, teacher_resid, w_out, projection, student_in, gate_act, up_act, w_down):
    def vmem(*shape, dtype=BF16):
        return pltpu.VMEM(shape, dtype)

    return pl.pallas_call(
        kernel,
        out_shape=(
            jax.ShapeDtypeStruct((TOK, FF), F32),
            jax.ShapeDtypeStruct((TOK, FF), F32),
            jax.ShapeDtypeStruct((FF, DC), F32),
        ),
        in_specs=[pl.BlockSpec(memory_space=pl.ANY)] * 8,
        out_specs=(pl.BlockSpec(memory_space=pltpu.VMEM),) * 3,
        scratch_shapes=[
            vmem(Q, 4, 2, 2, S, DK),
            vmem(Q, 4, 4, S, DK),
            vmem(Q, 2, 2, S, DK),
            vmem(Q, 2, 4, S, DK),
            vmem(Q, 4, S, DK),
            vmem(Q, 3, S, DK),
            vmem(Q, 4, 4, S, DK),
            vmem(Q, 4, 2, 2, S, DC),
            vmem(Q, 4, 2, S, DC),
            vmem(Q, 4, 2, S, DC),
            vmem(Q, 3, 2, S, DC),
            vmem(Q, 2, S, DC, dtype=F32),
            vmem(Q, 2, S, DC),
            vmem(Q, S, DC),
            vmem(Q, S, DS),
            vmem(Q, S, DC),
            vmem(2, 8, TOK, DC),
            vmem(TOK, FF),
            vmem(2, FF, 8 * TOK),
            vmem(4, 4, TOK, DC),
            vmem(2, 2, TOK, DC),
            vmem(2, 4, TOK, DC),
            vmem(4, TOK, DC),
            vmem(3, TOK, DC),
            vmem(TOK, DC, dtype=F32),
            vmem(DK, DK),
            vmem(DK, DC),
            vmem(FF, DS),
            vmem(TOK, DK),
            vmem(TOK, DC),
            vmem(TOK, FF),
            vmem(TOK, FF),
            pltpu.SemaphoreType.DMA((N_SLOTS,)),
            pltpu.SemaphoreType.DMA((N_SLOTS,)),
            pltpu.SemaphoreType.DMA((Q + 7,)),
        ],
        compiler_params=pltpu.CompilerParams(
            collective_id=0, has_side_effects=True, vmem_limit_bytes=58 * 2**20
        ),
        name="distill_step",
    )(attn_out, teacher_resid, w_out, projection, student_in, gate_act, up_act, w_down)


def solution(mesh):
    in_specs = (
        P("dp", "tensor"),
        P("tensor", "dp"),
        P("tensor", "dp"),
        P("dp", "tensor"),
        P("dp", "tensor"),
        P("dp", "tensor"),
        P("dp", "tensor"),
        P("tensor", None),
    )
    out_specs = (P("dp", "tensor"), P("dp", "tensor"), P("tensor", "dp"))
    return jax.shard_map(
        per_device, mesh=mesh, in_specs=in_specs, out_specs=out_specs, check_vma=False
    )
```

```python
import functools

import jax
import jax.numpy as jnp
from jax import lax
from jax.experimental import pallas as pl
from jax.experimental.pallas import tpu as pltpu
from jax.sharding import PartitionSpec as P

MESH = pl.DeviceIdType.MESH
F32 = jnp.float32
BF16 = jnp.bfloat16

Q = 4
TOK = 128
S = TOK // Q
DK = 1024
DC = 256
DS = 4096
FF = 896
ORDER = ("own.0", "own.1", "student", "far.0", "own.2", "turn", "sib.0", "far.1", "own.3", "hown", "stf", "far.2", "mix.0", "sib.1", "stz", "far.3", "mix.1", "fwd.0", "fwd.1", "hfar", "z.0", "sib.2", "ste", "z.1", "mix.2", "sib.3", "state.0", "mix.3", "fwd.2", "state.1", "hsib", "fwd.3", "hend", "ally.0", "z.2", "ally.1", "z.3", "state.2", "allf.0", "map.0", "allf.1", "map.1", "state.3", "tgt.0", "tx.0", "ally.2", "tgt.1", "tx.1", "tz.0", "ally.3", "allf.2", "tz.1", "map.2", "mis.0", "mis.1", "mir.0", "ey.0", "allf.3", "map.3", "mir.1", "ey.1", "fy.0", "tgt.2", "fy.1", "ef.0", "tx.2", "tgt.3", "ef.1", "tz.2", "tx.3", "ff.0", "mis.2", "ff.1", "ee.0", "ee.1", "tz.3", "fe.0", "fe.1", "ey.2", "mir.2", "mis.3", "fy.2", "ef.2", "mir.3", "ey.3", "ff.2", "fy.3", "ee.2", "ef.3", "fe.2", "ff.3", "ee.3", "grads", "fe.3", "down")

A_SLOTS, B_SLOTS, C_SLOTS, D_SLOTS, E_SLOTS = 12, 9, 13, 5, 15
E_GATHER = 7
A0 = 0
B0 = A0 + A_SLOTS * Q
C0 = B0 + B_SLOTS * Q
D0 = C0 + C_SLOTS * Q
E0 = D0 + D_SLOTS * Q
SB0 = E0 + E_SLOTS * Q
H0 = SB0 + B_SLOTS
N_SLOTS = H0 + A_SLOTS


def kernel(
    attn, resid, w_out, proj, stud, gate, up, w_down,
    gate_grad, up_grad, down_grad,
    g, p1, y1, y2, r, zr, ta, p2, ds1, p3, dx, p4, p4b, dz,
    ma, mt, mb, hid, ht, sp, sy1, sy2, sr, szr, so,
    vw_out, vproj, vw_down, vturned, vresid, vstud, vgate, vup,
    ss, rs, ls,
):
    d = lax.axis_index("dp")
    t = lax.axis_index("tensor")
    x, zh, c = d // 4, lax.rem(d // 2, 2), lax.rem(d, 2)
    y, zl = t // 4, lax.rem(t, 4)

    def dev(x_, zh_, c_, y_, zl_):
        return ((x_ * 2 + zh_) * 2 + c_, y_ * 4 + zl_)

    def ring(a, k):
        return lax.rem(a + k, 4)

    sib = dev(x, zh, 1 - c, y, zl)
    far = dev(x, 1 - zh, c, y, zl)
    xs = [dev(ring(x, k), zh, c, y, zl) for k in (1, 2, 3)]
    zs = [dev(x, zh, c, y, ring(zl, k)) for k in (1, 2, 3)]
    yn, yp = dev(x, zh, c, ring(y, 1), zl), dev(x, zh, c, ring(y, 3), zl)
    mirror = (t, d)

    def load(i, src, dst):
        return pltpu.make_async_copy(src, dst, ls.at[i])

    own_a = [load(q, attn.at[pl.ds(q * S, S)], g.at[q, x, zh, c]) for q in range(Q)]
    l_gate = load(Q, gate, vgate)
    l_up = load(Q + 1, up, vup)
    l_down = load(Q + 2, w_down, vw_down)
    l_out = load(Q + 3, w_out, vw_out)
    l_proj = load(Q + 4, proj, vproj)
    l_resid = load(Q + 5, resid, vresid)
    l_stud = load(Q + 6, stud, vstud)
    for cp in [l_gate, l_up, l_down, l_out] + own_a + [l_proj, l_resid, l_stud]:
        cp.start()

    barrier = pltpu.get_barrier_semaphore()
    for peer in [sib, far, yn, yp] + xs + zs:
        pl.semaphore_signal(barrier, 1, device_id=peer, device_id_type=MESH)

    @pl.when(d != t)
    def _():
        pl.semaphore_signal(barrier, 1, device_id=mirror, device_id_type=MESH)

    pl.semaphore_wait(barrier, jnp.where(d != t, 11, 10))

    started = []

    def send(slot, src, dst, peer):
        cp = pltpu.make_async_remote_copy(
            src, dst, ss.at[slot], rs.at[slot], device_id=peer, device_id_type=MESH
        )
        cp.start()
        started.append(cp)
        return cp

    def gather_dp_own(base, own, place, place2):
        dst = place(x, zh, c)
        m = {}
        m["z"] = send(base, own, dst, far)
        for k in (1, 2, 3):
            m["x", k] = send(base + k, own, dst, xs[k - 1])
        m["s0"] = send(base + 4, own, dst, sib)
        return m

    def gather_dp_far(base, m, place, place2):
        m["z"].wait_recv()
        piece = place(x, 1 - zh, c)
        for k in (1, 2, 3):
            m["zx", k] = send(base + 4 + k, piece, piece, xs[k - 1])
        m["s1"] = send(base + 8, piece, piece, sib)

    def gather_dp_sib(base, m, place, place2):
        for k in (1, 3, 2):
            m["x", k].wait_recv()
            m["zx", k].wait_recv()
            piece = place2(ring(x, 4 - k), c)
            m["s", k] = send(base + 8 + k, piece, piece, sib)

    def gather_dp_end(m):
        m["s0"].wait_recv()
        m["s1"].wait_recv()
        for k in (1, 3, 2):
            m["s", k].wait_recv()

    def scatter_y_first(base, part, a1):
        far_y = ring(y, 2)
        m = {}
        m["h0"] = send(base, part.at[far_y, pl.ds(0, 2)], a1.at[0], yn)
        m["h1"] = send(base + 1, part.at[far_y, pl.ds(2, 2)], a1.at[1], yp)
        return m

    def scatter_y_raw(base, m, part, a2):
        m["r0"] = send(base + 2, part.at[ring(y, 1), pl.ds(2, 2)], a2.at[0, pl.ds(2, 2)], yn)
        m["r1"] = send(base + 3, part.at[ring(y, 3), pl.ds(0, 2)], a2.at[1, pl.ds(0, 2)], yp)

    def scatter_y_forward(base, m, part, a1, a2):
        for side, (lo, to, peer) in enumerate(((0, ring(y, 1), yn), (2, ring(y, 3), yp))):
            m["h%d" % side].wait_recv()
            for i in range(2):
                both = part[to, lo + i].astype(F32) + a1[side, i].astype(F32)
                part[to, lo + i] = both.astype(BF16)
            m["c%d" % side] = send(
                base + 4 + side, part.at[to, pl.ds(lo, 2)], a2.at[side, pl.ds(lo, 2)], peer
            )

    def scatter_z(base, m, part, a2, res, az):
        for n in ("r0", "r1", "c0", "c1"):
            m[n].wait_recv()
        for i in range(4):
            total = part[y, i].astype(F32) + a2[0, i].astype(F32) + a2[1, i].astype(F32)
            res[i] = total.astype(BF16)
        for k in (1, 2, 3):
            m["z", k] = send(base + 5 + k, res.at[ring(zl, k)], az.at[k - 1], zs[k - 1])

    def scatter_end(m, res, az):
        for k in (1, 2, 3):
            m["z", k].wait_recv()
        total = res[zl].astype(F32)
        for k in range(3):
            total += az[k].astype(F32)
        return total

    def gather_z(base, view, early=False):
        own = view(y, zl, 1)
        m = {("z", k): send(base + k - 1, own, own, zs[k - 1]) for k in (1, 2, 3)}
        m["early"] = early
        if early:
            m["y0", 0] = send(base + 3, own, own, yn)
            m["y1", 0] = send(base + 4, own, own, yp)
        return m

    def gather_y(base, m, view):
        if m["early"]:
            for k in (1, 3, 2):
                m["z", k].wait_recv()
                piece = view(y, ring(zl, 4 - k), 1)
                m["y0", k] = send(base + 3 + 2 * k, piece, piece, yn)
                m["y1", k] = send(base + 4 + 2 * k, piece, piece, yp)
        else:
            for k in (1, 2, 3):
                m["z", k].wait_recv()
            mine = view(y, 0, 4)
            m["y0", 0] = send(base + 3, mine, mine, yn)
            m["y1", 0] = send(base + 4, mine, mine, yp)

    def gather_forward(base, m, view):
        base += 11 if m["early"] else 5
        for side, (far_y, lo, peer) in enumerate(((ring(y, 3), 0, yn), (ring(y, 1), 2, yp))):
            for k in (0, 1, 3, 2) if m["early"] else (0,):
                m["y%d" % side, k].wait_recv()
            half = view(far_y, lo, 2)
            m["f%d" % side] = send(base + side, half, half, peer)

    def gather_end(m):
        m["f0"].wait_recv()
        m["f1"].wait_recv()

    A = [None] * Q
    B = [None] * Q
    C = [None] * Q
    D = [{} for _ in range(Q)]
    E = [None] * Q
    EM = [None] * Q

    def g_place(q):
        return lambda x_, zh_, c_: g.at[q, x_, zh_, c_]

    def g_place2(q):
        return lambda x_, c_: g.at[q, x_, :, c_]

    def ta_view(q):
        return lambda y_, lo, n: ta.at[q, y_, pl.ds(lo, n)]

    def ma_view(q):
        def view(y_, lo, n):
            start = pl.multiple_of((y_ * 4 + lo) * DC, DC)
            return ma.at[pl.ds(q * S, S), pl.ds(start, n * DC)]

        return view

    def mb_view(q):
        rows = pl.ds(q * S, S)

        def view(y_, lo, n):
            if n == 1:
                return mb.at[lax.rem(lo, 2), y_ * 2 + lo // 2, rows]
            if n == 2:
                return mb.at[:, y_ * 2 + lo // 2, rows]
            return mb.at[:, pl.ds(y_ * 2, 2), rows]

        return view

    def mix(q):
        def cols(n, _):
            at = pl.ds(pl.multiple_of(n * 256, 256), 256)
            out = jnp.dot(g[q].reshape(16 * S, DK), vw_out[:, at], preferred_element_type=F32)
            p1[q, :, :, :, at] = out.astype(BF16).reshape(4, 4, S, 256)
            return 0

        lax.fori_loop(0, DK // 256, cols, 0)

    def map_target(q, yg):
        out = jnp.dot(ta[q, yg].reshape(4 * S, DK), vproj[...], preferred_element_type=F32)
        p2[q, yg] = out.astype(BF16).reshape(2, 2, S, DC)

    def s_far(q):
        gather_dp_far(A0 + A_SLOTS * q, A[q], g_place(q), g_place2(q))

    def s_sib(q):
        gather_dp_sib(A0 + A_SLOTS * q, A[q], g_place(q), g_place2(q))

    def s_own(q):
        base = A0 + A_SLOTS * q
        A[q] = gather_dp_own(base, attn.at[pl.ds(q * S, S)], g_place(q), g_place2(q))

    def s_mix(q):
        own_a[q].wait()
        gather_dp_end(A[q])
        mix(q)
        B[q] = scatter_y_first(B0 + B_SLOTS * q, p1.at[q], y1.at[q])
        scatter_y_raw(B0 + B_SLOTS * q, B[q], p1.at[q], y2.at[q])

    def s_forward(q):
        scatter_y_forward(B0 + B_SLOTS * q, B[q], p1.at[q], y1.at[q], y2.at[q])

    def s_z(q):
        scatter_z(B0 + B_SLOTS * q, B[q], p1.at[q], y2.at[q], r.at[q], zr.at[q])

    def s_state(q):
        total = scatter_end(B[q], r.at[q], zr.at[q])
        state = total + vresid[pl.ds(q * S, S)].astype(F32)
        ta[q, y, zl] = state.astype(BF16)
        C[q] = gather_z(C0 + C_SLOTS * q, ta_view(q), early=True)

    def s_all_y(q):
        gather_y(C0 + C_SLOTS * q, C[q], ta_view(q))

    def s_all_forward(q):
        gather_forward(C0 + C_SLOTS * q, C[q], ta_view(q))

    def s_map(q):
        map_target(q, y)
        map_target(q, ring(y, 1))
        map_target(q, ring(y, 3))

    def s_target(q):
        gather_end(C[q])
        map_target(q, ring(y, 2))
        D[q]["s"] = send(D0 + D_SLOTS * q, p2.at[q, :, :, 1 - c], ds1.at[q], sib)

    def s_target_x(q):
        D[q]["s"].wait_recv()
        for i in range(4):
            for j in range(2):
                p3[q, i, j] = (p2[q, i, j, c].astype(F32) + ds1[q, i, j].astype(F32)).astype(BF16)
        for k in (1, 2, 3):
            D[q]["x", k] = send(D0 + D_SLOTS * q + k, p3.at[q, ring(x, k)], dx.at[q, k - 1], xs[k - 1])

    def s_target_z(q):
        for k in (1, 2, 3):
            D[q]["x", k].wait_recv()
        total = p3[q, x].astype(F32)
        for k in range(3):
            total += dx[q, k].astype(F32)
        p4[q] = total
        p4b[q] = total.astype(BF16)
        D[q]["z"] = send(D0 + D_SLOTS * q + 4, p4b.at[q, 1 - zh], dz.at[q], far)

    def s_mismatch(q):
        D[q]["z"].wait_recv()
        rows = pl.ds(q * S, S)
        target = p4[q, zh] + dz[q].astype(F32)
        diff = (vstud[rows].astype(F32) + so[rows] - target).astype(BF16)
        mt[q] = diff
        col = pl.multiple_of(t * DC, DC)
        ma[rows, pl.ds(col, DC)] = diff
        base = E0 + E_SLOTS * q
        cp = pltpu.make_async_remote_copy(
            mt.at[q], mb_view(q)(y, zl, 1), ss.at[base + 2 * E_GATHER], rs.at[base + 2 * E_GATHER],
            device_id=mirror, device_id_type=MESH,
        )

        @pl.when(d != t)
        def _():
            pltpu.make_async_remote_copy(
                mt.at[q], mb.at[lax.rem(d, 2), d // 2, rows], ss.at[base + 2 * E_GATHER], rs.at[base + 2 * E_GATHER],
                device_id=mirror, device_id_type=MESH,
            ).start()

        @pl.when(d == t)
        def _():
            mb[lax.rem(d, 2), d // 2, rows] = diff

        EM[q] = cp
        E[q] = gather_z(base, ma_view(q))

    def s_mirror(q):
        @pl.when(d != t)
        def _():
            EM[q].wait()

        base = E0 + E_SLOTS * q + E_GATHER
        EM[q] = gather_z(base, mb_view(q))

    def s_ey(q):
        gather_y(E0 + E_SLOTS * q, E[q], ma_view(q))

    def s_fy(q):
        gather_y(E0 + E_SLOTS * q + E_GATHER, EM[q], mb_view(q))

    def s_ef(q):
        gather_forward(E0 + E_SLOTS * q, E[q], ma_view(q))

    def s_ff(q):
        gather_forward(E0 + E_SLOTS * q + E_GATHER, EM[q], mb_view(q))

    def s_ee(q):
        gather_end(E[q])

    def s_fe(q):
        gather_end(EM[q])

    st = {}

    def ht_place(x_, zh_, c_):
        return ht.at[c_, :, pl.ds(pl.multiple_of((x_ * 2 + zh_) * TOK, TOK), TOK)]

    def ht_place2(x_, c_):
        return ht.at[c_, :, pl.ds(pl.multiple_of(x_ * 2 * TOK, 2 * TOK), 2 * TOK)]

    def student():
        l_gate.wait()
        l_up.wait()
        gf = vgate[...].astype(F32)
        h = (gf * jax.nn.sigmoid(gf) * vup[...].astype(F32)).astype(BF16)
        hid[...] = h
        l_down.wait()

        def cols(i, _):
            at = pl.ds(pl.multiple_of(i * DC, DC), DC)
            out = jnp.dot(hid[...], vw_down[:, at], preferred_element_type=F32)
            sp[i // 4, lax.rem(i, 4)] = out.astype(BF16)
            return 0

        lax.fori_loop(0, DS // DC, cols, 0)
        st["m"] = scatter_y_first(SB0, sp, sy1)
        scatter_y_raw(SB0, st["m"], sp, sy2)
        ht[c, :, pl.ds(pl.multiple_of((x * 2 + zh) * TOK, TOK), TOK)] = h.astype(F32).T.astype(BF16)

    def student_forward():
        scatter_y_forward(SB0, st["m"], sp, sy1, sy2)

    def student_z():
        scatter_z(SB0, st["m"], sp, sy2, sr, szr)

    def student_end():
        so[...] = scatter_end(st["m"], sr, szr)

    def hidden_own():
        st["h"] = gather_dp_own(H0, ht_place(x, zh, c), ht_place, ht_place2)

    def hidden_far():
        gather_dp_far(H0, st["h"], ht_place, ht_place2)

    def hidden_end():
        gather_dp_end(st["h"])

    def hidden_sib():
        gather_dp_sib(H0, st["h"], ht_place, ht_place2)

    def turn():
        def block(i, _):
            at = pl.ds(pl.multiple_of(i * 128, 128), 128)
            vturned[at, :] = vw_down[:, at].T
            return 0

        lax.fori_loop(0, DS // 128, block, 0)

    def gate_up():
        def cols(i, _):
            at = pl.ds(pl.multiple_of(i * 128, 128), 128)
            hg = jnp.dot(ma[...], vturned[:, at], preferred_element_type=F32)
            gf = vgate[:, at].astype(F32)
            uf = vup[:, at].astype(F32)
            sg = jax.nn.sigmoid(gf)
            gate_grad[:, at] = hg * uf * sg * (1.0 + gf * (1.0 - sg))
            up_grad[:, at] = hg * gf * sg
            return 0

        lax.fori_loop(0, FF // 128, cols, 0)

    def down():
        def block(i, _):
            at = pl.ds(pl.multiple_of(i * 448, 64), 448)
            out = jnp.dot(ht[0, at], mb[0].reshape(8 * TOK, DC), preferred_element_type=F32)
            out += jnp.dot(ht[1, at], mb[1].reshape(8 * TOK, DC), preferred_element_type=F32)
            down_grad[at] = out
            return 0

        lax.fori_loop(0, FF // 448, block, 0)

    waited = set()

    def once(cp):
        if id(cp) not in waited:
            waited.add(id(cp))
            cp.wait()

    steps = {
        "own": s_own, "far": s_far, "sib": s_sib, "mix": s_mix, "fwd": s_forward,
        "z": s_z, "state": s_state, "ally": s_all_y, "allf": s_all_forward, "map": s_map,
        "tgt": s_target, "tx": s_target_x, "tz": s_target_z, "mis": s_mismatch, "mir": s_mirror,
        "ey": s_ey, "fy": s_fy, "ef": s_ef, "ff": s_ff, "ee": s_ee, "fe": s_fe,
        "student": student, "stf": student_forward, "stz": student_z, "ste": student_end,
        "hown": hidden_own, "hfar": hidden_far, "hsib": hidden_sib, "hend": hidden_end,
        "turn": turn, "grads": gate_up, "down": down,
    }
    before = {"mix": l_out, "state": l_resid, "map": l_proj, "mis": l_stud}
    for step in ORDER:
        name, _, q = step.partition(".")
        if name in before:
            once(before[name])
        if q:
            steps[name](int(q))
        else:
            steps[name]()
    for cp in started:
        cp.wait_send()


def hand_out(a, b, c, a_out, b_out, c_out):
    a_out[...] = a[...]
    b_out[...] = b[...]
    c_out[...] = c[...]


def per_device(attn_out, teacher_resid, w_out, projection, student_in, gate_act, up_act, w_down):
    def vmem(*shape, dtype=BF16):
        return pltpu.VMEM(shape, dtype)

    grads = pl.pallas_call(
        kernel,
        out_shape=(
            jax.ShapeDtypeStruct((TOK, FF), F32),
            jax.ShapeDtypeStruct((TOK, FF), F32),
            jax.ShapeDtypeStruct((FF, DC), F32),
        ),
        in_specs=[pl.BlockSpec(memory_space=pl.ANY)] * 8,
        out_specs=(pl.BlockSpec(memory_space=pltpu.VMEM),) * 3,
        scratch_shapes=[
            vmem(Q, 4, 2, 2, S, DK),
            vmem(Q, 4, 4, S, DK),
            vmem(Q, 2, 2, S, DK),
            vmem(Q, 2, 4, S, DK),
            vmem(Q, 4, S, DK),
            vmem(Q, 3, S, DK),
            vmem(Q, 4, 4, S, DK),
            vmem(Q, 4, 2, 2, S, DC),
            vmem(Q, 4, 2, S, DC),
            vmem(Q, 4, 2, S, DC),
            vmem(Q, 3, 2, S, DC),
            vmem(Q, 2, S, DC, dtype=F32),
            vmem(Q, 2, S, DC),
            vmem(Q, S, DC),
            vmem(TOK, DS),
            vmem(Q, S, DC),
            vmem(2, 8, TOK, DC),
            vmem(TOK, FF),
            vmem(2, FF, 8 * TOK),
            vmem(4, 4, TOK, DC),
            vmem(2, 2, TOK, DC),
            vmem(2, 4, TOK, DC),
            vmem(4, TOK, DC),
            vmem(3, TOK, DC),
            vmem(TOK, DC, dtype=F32),
            vmem(DK, DK),
            vmem(DK, DC),
            vmem(FF, DS),
            vmem(DS, FF),
            vmem(TOK, DK),
            vmem(TOK, DC),
            vmem(TOK, FF),
            vmem(TOK, FF),
            pltpu.SemaphoreType.DMA((N_SLOTS,)),
            pltpu.SemaphoreType.DMA((N_SLOTS,)),
            pltpu.SemaphoreType.DMA((Q + 7,)),
        ],
        compiler_params=pltpu.CompilerParams(
            collective_id=0, has_side_effects=True, vmem_limit_bytes=58 * 2**20
        ),
        name="distill_step",
    )(attn_out, teacher_resid, w_out, projection, student_in, gate_act, up_act, w_down)
    return pl.pallas_call(
        hand_out,
        out_shape=tuple(jax.ShapeDtypeStruct(g.shape, g.dtype) for g in grads),
        in_specs=[pl.BlockSpec(memory_space=pltpu.VMEM)] * 3,
        out_specs=(pl.BlockSpec(memory_space=pltpu.VMEM),) * 3,
        name="hand_out",
    )(*grads)


def solution(mesh):
    in_specs = (
        P("dp", "tensor"),
        P("tensor", "dp"),
        P("tensor", "dp"),
        P("dp", "tensor"),
        P("dp", "tensor"),
        P("dp", "tensor"),
        P("dp", "tensor"),
        P("tensor", None),
    )
    out_specs = (P("dp", "tensor"), P("dp", "tensor"), P("tensor", "dp"))
    return jax.shard_map(
        per_device, mesh=mesh, in_specs=in_specs, out_specs=out_specs, check_vma=False
    )
```

```python
import functools

import jax
import jax.numpy as jnp
from jax import lax
from jax.experimental import pallas as pl
from jax.experimental.pallas import tpu as pltpu
from jax.sharding import PartitionSpec as P

MESH = pl.DeviceIdType.MESH
F32 = jnp.float32
BF16 = jnp.bfloat16

Q = 4
TOK = 128
S = TOK // Q
DK = 1024
DC = 256
DS = 4096
FF = 896
ORDER = ("own.0", "hide", "sta", "far.0", "own.1", "own.2", "student", "sib.0", "far.1", "own.3", "mix.0", "sib.1", "far.2", "far.3", "hown", "fwd.0", "mix.1", "z.0", "sib.3", "fwd.1", "mix.3", "z.1", "hfar", "sib.2", "state.0", "fwd.3", "mix.2", "state.1", "fwd.2", "z.3", "stf", "ally.0", "z.2", "ally.1", "turn", "state.3", "allf.0", "allf.1", "state.2", "map.1", "hsib", "map.0", "tgt.0", "ally.3", "tgt.1", "stz", "ally.2", "tz.0", "allf.3", "tz.1", "ste", "allf.2", "mis.1", "map.2", "map.3", "tgt.3", "mis.0", "tgt.2", "hend", "ey.1", "fy.1", "ey.0", "tz.3", "fy.0", "ef.1", "tz.2", "ff.1", "mis.3", "ef.0", "ff.0", "fe.1", "mis.2", "ey.3", "fy.3", "ey.2", "fe.0", "fy.2", "ee.1", "ff.3", "ef.3", "ef.2", "ff.2", "ee.3", "fe.3", "ee.0", "ee.2", "grads", "fe.2", "down")

A_SLOTS, B_SLOTS, C_SLOTS, D_SLOTS, E_SLOTS = 12, 9, 13, 8, 15
E_GATHER = 4
E_MIRROR = 11
A0 = 0
B0 = A0 + A_SLOTS * Q
C0 = B0 + B_SLOTS * Q
D0 = C0 + C_SLOTS * Q
E0 = D0 + D_SLOTS * Q
SB0 = E0 + E_SLOTS * Q
H0 = SB0 + B_SLOTS
N_SLOTS = H0 + A_SLOTS


def kernel(
    attn, resid, w_out, proj, stud, gate, up, w_down,
    gate_grad, up_grad, down_grad,
    g, p1, y1, y2, r, zr, ta, p2, dx, p4, p4b, dz,
    ma, mt, mb, hid, ht, sp, sy1, sy2, sr, szr, so,
    vw_out, vproj, vw_down, vturned, vresid, vstud, vgate, vup,
    ss, rs, ls,
):
    d = lax.axis_index("dp")
    t = lax.axis_index("tensor")
    x, zh, c = d // 4, lax.rem(d // 2, 2), lax.rem(d, 2)
    y, zl = t // 4, lax.rem(t, 4)

    def dev(x_, zh_, c_, y_, zl_):
        return ((x_ * 2 + zh_) * 2 + c_, y_ * 4 + zl_)

    def ring(a, k):
        return lax.rem(a + k, 4)

    sib = dev(x, zh, 1 - c, y, zl)
    far = dev(x, 1 - zh, c, y, zl)
    xs = [dev(ring(x, k), zh, c, y, zl) for k in (1, 2, 3)]
    zs = [dev(x, zh, c, y, ring(zl, k)) for k in (1, 2, 3)]
    yn, yp = dev(x, zh, c, ring(y, 1), zl), dev(x, zh, c, ring(y, 3), zl)
    xo = [dev(ring(x, k), zh, 1 - c, y, zl) for k in (1, 2, 3)]
    mirror_to = [(t, (d // 4) * 4 + k) for k in range(4)]
    mirror_from = [((t // 4) * 4 + k, d) for k in range(4)]
    other = [jnp.logical_or(d != t, lax.rem(d, 4) != k) for k in range(4)]

    def load(i, src, dst):
        return pltpu.make_async_copy(src, dst, ls.at[i])

    own_a = [load(q, attn.at[pl.ds(q * S, S)], g.at[q, x, zh, c]) for q in range(Q)]
    l_gate = load(Q, gate, vgate)
    l_up = load(Q + 1, up, vup)
    l_down = load(Q + 2, w_down, vw_down)
    l_out = load(Q + 3, w_out, vw_out)
    l_proj = load(Q + 4, proj, vproj)
    l_resid = load(Q + 5, resid, vresid)
    l_stud = load(Q + 6, stud, vstud)
    for cp in [l_gate, l_up, l_down, l_out] + own_a + [l_proj, l_resid, l_stud]:
        cp.start()

    barrier = pltpu.get_barrier_semaphore()
    for peer in [sib, far, yn, yp] + xs + xo + zs:
        pl.semaphore_signal(barrier, 1, device_id=peer, device_id_type=MESH)
    for k in range(4):

        @pl.when(other[k])
        def _():
            pl.semaphore_signal(barrier, 1, device_id=mirror_from[k], device_id_type=MESH)

    pl.semaphore_wait(barrier, jnp.where(d != t, 17, 16))

    started = []

    def send(slot, src, dst, peer):
        cp = pltpu.make_async_remote_copy(
            src, dst, ss.at[slot], rs.at[slot], device_id=peer, device_id_type=MESH
        )
        cp.start()
        started.append(cp)
        return cp

    def gather_dp_own(base, own, place, place2):
        dst = place(x, zh, c)
        m = {}
        m["z"] = send(base, own, dst, far)
        for k in (1, 2, 3):
            m["x", k] = send(base + k, own, dst, xs[k - 1])
        m["s0"] = send(base + 4, own, dst, sib)
        return m

    def gather_dp_far(base, m, place, place2):
        m["z"].wait_recv()
        piece = place(x, 1 - zh, c)
        for k in (1, 2, 3):
            m["zx", k] = send(base + 4 + k, piece, piece, xs[k - 1])
        m["s1"] = send(base + 8, piece, piece, sib)

    def gather_dp_sib(base, m, place, place2):
        for k in (1, 3, 2):
            m["x", k].wait_recv()
            m["zx", k].wait_recv()
            piece = place2(ring(x, 4 - k), c)
            m["s", k] = send(base + 8 + k, piece, piece, sib)

    def gather_dp_end(m):
        m["s0"].wait_recv()
        m["s1"].wait_recv()
        for k in (1, 3, 2):
            m["s", k].wait_recv()

    def scatter_y_first(base, part, a1):
        far_y = ring(y, 2)
        m = {}
        m["h0"] = send(base, part.at[far_y, pl.ds(0, 2)], a1.at[0], yn)
        m["h1"] = send(base + 1, part.at[far_y, pl.ds(2, 2)], a1.at[1], yp)
        return m

    def scatter_y_raw(base, m, part, a2):
        m["r0"] = send(base + 2, part.at[ring(y, 1), pl.ds(2, 2)], a2.at[0, pl.ds(2, 2)], yn)
        m["r1"] = send(base + 3, part.at[ring(y, 3), pl.ds(0, 2)], a2.at[1, pl.ds(0, 2)], yp)

    def scatter_y_forward(base, m, part, a1, a2):
        for side, (lo, to, peer) in enumerate(((0, ring(y, 1), yn), (2, ring(y, 3), yp))):
            m["h%d" % side].wait_recv()
            for i in range(2):
                both = part[to, lo + i].astype(F32) + a1[side, i].astype(F32)
                part[to, lo + i] = both.astype(BF16)
            m["c%d" % side] = send(
                base + 4 + side, part.at[to, pl.ds(lo, 2)], a2.at[side, pl.ds(lo, 2)], peer
            )

    def scatter_z(base, m, part, a2, res, az):
        for n in ("r0", "r1", "c0", "c1"):
            m[n].wait_recv()
        for i in range(4):
            total = part[y, i].astype(F32) + a2[0, i].astype(F32) + a2[1, i].astype(F32)
            res[i] = total.astype(BF16)
        for k in (1, 2, 3):
            m["z", k] = send(base + 5 + k, res.at[ring(zl, k)], az.at[k - 1], zs[k - 1])

    def scatter_end(m, res, az):
        for k in (1, 2, 3):
            m["z", k].wait_recv()
        total = res[zl].astype(F32)
        for k in range(3):
            total += az[k].astype(F32)
        return total

    def gather_z(base, view, early=False):
        own = view(y, zl, 1)
        m = {("z", k): send(base + k - 1, own, own, zs[k - 1]) for k in (1, 2, 3)}
        m["early"] = early
        if early:
            m["y0", 0] = send(base + 3, own, own, yn)
            m["y1", 0] = send(base + 4, own, own, yp)
        return m

    def gather_y(base, m, view):
        if m["early"]:
            for k in (1, 3, 2):
                m["z", k].wait_recv()
                piece = view(y, ring(zl, 4 - k), 1)
                m["y0", k] = send(base + 3 + 2 * k, piece, piece, yn)
                m["y1", k] = send(base + 4 + 2 * k, piece, piece, yp)
        else:
            for k in (1, 2, 3):
                if ("z", k) in m:
                    m["z", k].wait_recv()
            mine = view(y, 0, 4)
            m["y0", 0] = send(base + 3, mine, mine, yn)
            m["y1", 0] = send(base + 4, mine, mine, yp)

    def gather_forward(base, m, view):
        base += 11 if m["early"] else 5
        for side, (far_y, lo, peer) in enumerate(((ring(y, 3), 0, yn), (ring(y, 1), 2, yp))):
            for k in (0, 1, 3, 2) if m["early"] else (0,):
                m["y%d" % side, k].wait_recv()
            half = view(far_y, lo, 2)
            m["f%d" % side] = send(base + side, half, half, peer)

    def gather_end(m):
        m["f0"].wait_recv()
        m["f1"].wait_recv()

    A = [None] * Q
    B = [None] * Q
    C = [None] * Q
    D = [{} for _ in range(Q)]
    E = [None] * Q
    EM = [None] * Q

    def g_place(q):
        return lambda x_, zh_, c_: g.at[q, x_, zh_, c_]

    def g_place2(q):
        return lambda x_, c_: g.at[q, x_, :, c_]

    def ta_view(q):
        return lambda y_, lo, n: ta.at[q, y_, pl.ds(lo, n)]

    def ma_view(q):
        def view(y_, lo, n):
            start = pl.multiple_of((y_ * 4 + lo) * DC, DC)
            return ma.at[pl.ds(q * S, S), pl.ds(start, n * DC)]

        return view

    def mb_view(q):
        rows = pl.ds(q * S, S)

        def view(y_, lo, n):
            if n == 1:
                return mb.at[lax.rem(lo, 2), y_ * 2 + lo // 2, rows]
            if n == 2:
                return mb.at[:, y_ * 2 + lo // 2, rows]
            return mb.at[:, pl.ds(y_ * 2, 2), rows]

        return view

    def mix(q):
        def cols(n, _):
            at = pl.ds(pl.multiple_of(n * 256, 256), 256)
            out = jnp.dot(g[q].reshape(16 * S, DK), vw_out[:, at], preferred_element_type=F32)
            p1[q, :, :, :, at] = out.astype(BF16).reshape(4, 4, S, 256)
            return 0

        lax.fori_loop(0, DK // 256, cols, 0)

    def map_target(q, yg):
        out = jnp.dot(ta[q, yg].reshape(4 * S, DK), vproj[...], preferred_element_type=F32)
        p2[q, yg] = out.astype(BF16).reshape(2, 2, S, DC)

    def s_far(q):
        gather_dp_far(A0 + A_SLOTS * q, A[q], g_place(q), g_place2(q))

    def s_sib(q):
        gather_dp_sib(A0 + A_SLOTS * q, A[q], g_place(q), g_place2(q))

    def s_own(q):
        base = A0 + A_SLOTS * q
        A[q] = gather_dp_own(base, attn.at[pl.ds(q * S, S)], g_place(q), g_place2(q))

    def s_mix(q):
        own_a[q].wait()
        gather_dp_end(A[q])
        mix(q)
        B[q] = scatter_y_first(B0 + B_SLOTS * q, p1.at[q], y1.at[q])
        scatter_y_raw(B0 + B_SLOTS * q, B[q], p1.at[q], y2.at[q])

    def s_forward(q):
        scatter_y_forward(B0 + B_SLOTS * q, B[q], p1.at[q], y1.at[q], y2.at[q])

    def s_z(q):
        scatter_z(B0 + B_SLOTS * q, B[q], p1.at[q], y2.at[q], r.at[q], zr.at[q])

    def s_state(q):
        total = scatter_end(B[q], r.at[q], zr.at[q])
        state = total + vresid[pl.ds(q * S, S)].astype(F32)
        ta[q, y, zl] = state.astype(BF16)
        C[q] = gather_z(C0 + C_SLOTS * q, ta_view(q), early=True)

    def s_all_y(q):
        gather_y(C0 + C_SLOTS * q, C[q], ta_view(q))

    def s_all_forward(q):
        gather_forward(C0 + C_SLOTS * q, C[q], ta_view(q))

    def s_map(q):
        map_target(q, y)
        map_target(q, ring(y, 1))
        map_target(q, ring(y, 3))

    def s_target(q):
        gather_end(C[q])
        map_target(q, ring(y, 2))
        base = D0 + D_SLOTS * q
        for k in (1, 3, 2):
            D[q][k - 1] = send(base + k - 1, p2.at[q, ring(x, k), :, c], dx.at[q, k - 1], xs[k - 1])
            D[q][k + 2] = send(base + k + 2, p2.at[q, ring(x, k), :, 1 - c], dx.at[q, k + 2], xo[k - 1])
        D[q][6] = send(base + 6, p2.at[q, x, :, 1 - c], dx.at[q, 6], sib)

    def s_target_z(q):
        for k in range(7):
            D[q][k].wait_recv()
        total = p2[q, x, :, c].astype(F32)
        for k in range(7):
            total += dx[q, k].astype(F32)
        p4[q] = total
        p4b[q] = total.astype(BF16)
        D[q]["z"] = send(D0 + D_SLOTS * q + 7, p4b.at[q, 1 - zh], dz.at[q], far)

    def s_mismatch(q):
        D[q]["z"].wait_recv()
        rows = pl.ds(q * S, S)
        target = p4[q, zh] + dz[q].astype(F32)
        diff = (vstud[rows].astype(F32) + so[rows] - target).astype(BF16)
        mt[q] = diff
        col = pl.multiple_of(t * DC, DC)
        ma[rows, pl.ds(col, DC)] = diff
        base = E0 + E_SLOTS * q
        for k in range(4):

            @pl.when(other[k])
            def _():
                mirror_copy(q, k, lax.rem(d, 4), d).start()

        @pl.when(d == t)
        def _():
            mb[lax.rem(d, 2), d // 2, rows] = diff

        E[q] = gather_z(base, ma_view(q))

    def mirror_copy(q, k, slot, owner):
        base = E0 + E_SLOTS * q + E_MIRROR
        return pltpu.make_async_remote_copy(
            mt.at[q], mb.at[lax.rem(owner, 2), owner // 2, pl.ds(q * S, S)],
            ss.at[base + k], rs.at[base + slot],
            device_id=mirror_to[k], device_id_type=MESH,
        )

    def s_ey(q):
        gather_y(E0 + E_SLOTS * q, E[q], ma_view(q))

    def s_fy(q):
        for k in range(4):

            @pl.when(other[k])
            def _():
                mirror_copy(q, k, k, (t // 4) * 4 + k).wait_recv()

        EM[q] = {"early": False}
        gather_y(E0 + E_SLOTS * q + E_GATHER, EM[q], mb_view(q))

    def s_ef(q):
        gather_forward(E0 + E_SLOTS * q, E[q], ma_view(q))

    def s_ff(q):
        gather_forward(E0 + E_SLOTS * q + E_GATHER, EM[q], mb_view(q))

    def s_ee(q):
        gather_end(E[q])

    def s_fe(q):
        gather_end(EM[q])
        for k in range(4):

            @pl.when(other[k])
            def _():
                mirror_copy(q, k, k, d).wait_send()

    st = {}

    def ht_place(x_, zh_, c_):
        return ht.at[c_, :, pl.ds(pl.multiple_of((x_ * 2 + zh_) * TOK, TOK), TOK)]

    def ht_place2(x_, c_):
        return ht.at[c_, :, pl.ds(pl.multiple_of(x_ * 2 * TOK, 2 * TOK), 2 * TOK)]

    def hide():
        l_gate.wait()
        l_up.wait()
        gf = vgate[...].astype(F32)
        h = (gf * jax.nn.sigmoid(gf) * vup[...].astype(F32)).astype(BF16)
        hid[...] = h
        ht[c, :, pl.ds(pl.multiple_of((x * 2 + zh) * TOK, TOK), TOK)] = h.astype(F32).T.astype(BF16)

    def student_part(first, last):
        def cols(i, _):
            at = pl.ds(pl.multiple_of(i * DC, DC), DC)
            out = jnp.dot(hid[...], vw_down[:, at], preferred_element_type=F32)
            sp[i // 4, lax.rem(i, 4)] = out.astype(BF16)
            return 0

        lax.fori_loop(first, last, cols, 0)

    def student_a():
        l_down.wait()
        student_part(0, 8)

    def student():
        student_part(8, 16)
        st["m"] = scatter_y_first(SB0, sp, sy1)
        scatter_y_raw(SB0, st["m"], sp, sy2)

    def student_forward():
        scatter_y_forward(SB0, st["m"], sp, sy1, sy2)

    def student_z():
        scatter_z(SB0, st["m"], sp, sy2, sr, szr)

    def student_end():
        so[...] = scatter_end(st["m"], sr, szr)

    def hidden_own():
        st["h"] = gather_dp_own(H0, ht_place(x, zh, c), ht_place, ht_place2)

    def hidden_far():
        gather_dp_far(H0, st["h"], ht_place, ht_place2)

    def hidden_end():
        gather_dp_end(st["h"])

    def hidden_sib():
        gather_dp_sib(H0, st["h"], ht_place, ht_place2)

    def turn():
        def block(i, _):
            at = pl.ds(pl.multiple_of(i * 128, 128), 128)
            vturned[at, :] = vw_down[:, at].T
            return 0

        lax.fori_loop(0, DS // 128, block, 0)

    def gate_up():
        def cols(i, _):
            at = pl.ds(pl.multiple_of(i * 128, 128), 128)
            hg = jnp.dot(ma[...], vturned[:, at], preferred_element_type=F32)
            gf = vgate[:, at].astype(F32)
            uf = vup[:, at].astype(F32)
            sg = jax.nn.sigmoid(gf)
            gate_grad[:, at] = hg * uf * sg * (1.0 + gf * (1.0 - sg))
            up_grad[:, at] = hg * gf * sg
            return 0

        lax.fori_loop(0, FF // 128, cols, 0)

    def down():
        def block(i, _):
            at = pl.ds(pl.multiple_of(i * 448, 64), 448)
            out = jnp.dot(ht[0, at], mb[0].reshape(8 * TOK, DC), preferred_element_type=F32)
            out += jnp.dot(ht[1, at], mb[1].reshape(8 * TOK, DC), preferred_element_type=F32)
            down_grad[at] = out
            return 0

        lax.fori_loop(0, FF // 448, block, 0)

    waited = set()

    def once(cp):
        if id(cp) not in waited:
            waited.add(id(cp))
            cp.wait()

    steps = {
        "own": s_own, "far": s_far, "sib": s_sib, "mix": s_mix, "fwd": s_forward,
        "z": s_z, "state": s_state, "ally": s_all_y, "allf": s_all_forward, "map": s_map,
        "tgt": s_target, "tz": s_target_z, "mis": s_mismatch,
        "ey": s_ey, "fy": s_fy, "ef": s_ef, "ff": s_ff, "ee": s_ee, "fe": s_fe,
        "hide": hide, "sta": student_a, "student": student, "stf": student_forward, "stz": student_z, "ste": student_end,
        "hown": hidden_own, "hfar": hidden_far, "hsib": hidden_sib, "hend": hidden_end,
        "turn": turn, "grads": gate_up, "down": down,
    }
    before = {"mix": l_out, "state": l_resid, "map": l_proj, "mis": l_stud}
    for step in ORDER:
        name, _, q = step.partition(".")
        if name in before:
            once(before[name])
        if q:
            steps[name](int(q))
        else:
            steps[name]()
    for cp in started:
        cp.wait_send()


def hand_out(a, b, c, a_out, b_out, c_out):
    a_out[...] = a[...]
    b_out[...] = b[...]
    c_out[...] = c[...]


def per_device(attn_out, teacher_resid, w_out, projection, student_in, gate_act, up_act, w_down):
    def vmem(*shape, dtype=BF16):
        return pltpu.VMEM(shape, dtype)

    grads = pl.pallas_call(
        kernel,
        out_shape=(
            jax.ShapeDtypeStruct((TOK, FF), F32),
            jax.ShapeDtypeStruct((TOK, FF), F32),
            jax.ShapeDtypeStruct((FF, DC), F32),
        ),
        in_specs=[pl.BlockSpec(memory_space=pl.ANY)] * 8,
        out_specs=(pl.BlockSpec(memory_space=pltpu.VMEM),) * 3,
        scratch_shapes=[
            vmem(Q, 4, 2, 2, S, DK),
            vmem(Q, 4, 4, S, DK),
            vmem(Q, 2, 2, S, DK),
            vmem(Q, 2, 4, S, DK),
            vmem(Q, 4, S, DK),
            vmem(Q, 3, S, DK),
            vmem(Q, 4, 4, S, DK),
            vmem(Q, 4, 2, 2, S, DC),
            vmem(Q, 7, 2, S, DC),
            vmem(Q, 2, S, DC, dtype=F32),
            vmem(Q, 2, S, DC),
            vmem(Q, S, DC),
            vmem(TOK, DS),
            vmem(Q, S, DC),
            vmem(2, 8, TOK, DC),
            vmem(TOK, FF),
            vmem(2, FF, 8 * TOK),
            vmem(4, 4, TOK, DC),
            vmem(2, 2, TOK, DC),
            vmem(2, 4, TOK, DC),
            vmem(4, TOK, DC),
            vmem(3, TOK, DC),
            vmem(TOK, DC, dtype=F32),
            vmem(DK, DK),
            vmem(DK, DC),
            vmem(FF, DS),
            vmem(DS, FF),
            vmem(TOK, DK),
            vmem(TOK, DC),
            vmem(TOK, FF),
            vmem(TOK, FF),
            pltpu.SemaphoreType.DMA((N_SLOTS,)),
            pltpu.SemaphoreType.DMA((N_SLOTS,)),
            pltpu.SemaphoreType.DMA((Q + 7,)),
        ],
        compiler_params=pltpu.CompilerParams(
            collective_id=0, has_side_effects=True, vmem_limit_bytes=58 * 2**20
        ),
        name="distill_step",
    )(attn_out, teacher_resid, w_out, projection, student_in, gate_act, up_act, w_down)
    return pl.pallas_call(
        hand_out,
        out_shape=tuple(jax.ShapeDtypeStruct(g.shape, g.dtype) for g in grads),
        in_specs=[pl.BlockSpec(memory_space=pltpu.VMEM)] * 3,
        out_specs=(pl.BlockSpec(memory_space=pltpu.VMEM),) * 3,
        name="hand_out",
    )(*grads)


def solution(mesh):
    in_specs = (
        P("dp", "tensor"),
        P("tensor", "dp"),
        P("tensor", "dp"),
        P("dp", "tensor"),
        P("dp", "tensor"),
        P("dp", "tensor"),
        P("dp", "tensor"),
        P("tensor", None),
    )
    out_specs = (P("dp", "tensor"), P("dp", "tensor"), P("tensor", "dp"))
    return jax.shard_map(
        per_device, mesh=mesh, in_specs=in_specs, out_specs=out_specs, check_vma=False
    )
```

```python
import functools

import jax
import jax.numpy as jnp
from jax import lax
from jax.experimental import pallas as pl
from jax.experimental.pallas import tpu as pltpu
from jax.sharding import PartitionSpec as P

MESH = pl.DeviceIdType.MESH
F32 = jnp.float32
BF16 = jnp.bfloat16

Q = 4
TOK = 128
S = TOK // Q
DK = 1024
DC = 256
DS = 4096
FF = 896
ORDER = ("own.0", "hide", "sta", "far.0", "own.1", "own.2", "student", "sib.0", "far.1", "own.3", "mix.0", "sib.1", "far.2", "far.3", "hown", "fwd.0", "mix.1", "z.0", "sib.3", "fwd.1", "mix.3", "z.1", "hfar", "sib.2", "state.0", "fwd.3", "mix.2", "state.1", "fwd.2", "z.3", "stf", "ally.0", "z.2", "ally.1", "turn", "state.3", "allf.0", "allf.1", "state.2", "map.1", "hsib", "map.0", "tgt.0", "ally.3", "tgt.1", "stz", "ally.2", "tz.0", "allf.3", "tz.1", "ste", "allf.2", "mis.1", "map.2", "map.3", "tgt.3", "mis.0", "tgt.2", "hend", "ey.1", "fy.1", "ey.0", "tz.3", "fy.0", "ef.1", "tz.2", "ff.1", "mis.3", "ef.0", "ff.0", "fe.1", "mis.2", "ey.3", "fy.3", "ey.2", "fe.0", "fy.2", "ee.1", "ff.3", "ef.3", "ef.2", "ff.2", "ee.3", "fe.3", "ee.0", "ee.2", "grads", "fe.2", "down")

A_SLOTS, B_SLOTS, C_SLOTS, D_SLOTS, E_SLOTS = 12, 9, 13, 8, 15
E_GATHER = 4
E_MIRROR = 11
IN_FLIGHT = 60
A0 = 0
B0 = A0 + A_SLOTS * Q
C0 = B0 + B_SLOTS * Q
D0 = C0 + C_SLOTS * Q
E0 = D0 + D_SLOTS * Q
SB0 = E0 + E_SLOTS * Q
H0 = SB0 + B_SLOTS
N_SLOTS = H0 + A_SLOTS


def kernel(
    attn, resid, w_out, proj, stud, gate, up, w_down,
    gate_out, up_out, down_out,
    gate_grad, up_grad, down_grad, g, p1, y1, y2, r, zr, ta, p2, dx, p4, p4b, dz,
    ma, mt, mb, hid, ht, sp, sy1, sy2, sr, szr, so,
    vw_out, vproj, vw_down, vturned, vresid, vstud, vgate, vup,
    ss, rs, ls,
):
    d = lax.axis_index("dp")
    t = lax.axis_index("tensor")
    x, zh, c = d // 4, lax.rem(d // 2, 2), lax.rem(d, 2)
    y, zl = t // 4, lax.rem(t, 4)

    def dev(x_, zh_, c_, y_, zl_):
        return ((x_ * 2 + zh_) * 2 + c_, y_ * 4 + zl_)

    def ring(a, k):
        return lax.rem(a + k, 4)

    sib = dev(x, zh, 1 - c, y, zl)
    far = dev(x, 1 - zh, c, y, zl)
    xs = [dev(ring(x, k), zh, c, y, zl) for k in (1, 2, 3)]
    zs = [dev(x, zh, c, y, ring(zl, k)) for k in (1, 2, 3)]
    yn, yp = dev(x, zh, c, ring(y, 1), zl), dev(x, zh, c, ring(y, 3), zl)
    xo = [dev(ring(x, k), zh, 1 - c, y, zl) for k in (1, 2, 3)]
    mirror_to = [(t, (d // 4) * 4 + k) for k in range(4)]
    mirror_from = [((t // 4) * 4 + k, d) for k in range(4)]
    other = [jnp.logical_or(d != t, lax.rem(d, 4) != k) for k in range(4)]

    def load(i, src, dst):
        return pltpu.make_async_copy(src, dst, ls.at[i])

    own_a = [load(q, attn.at[pl.ds(q * S, S)], g.at[q, x, zh, c]) for q in range(Q)]
    l_gate = load(Q, gate, vgate)
    l_up = load(Q + 1, up, vup)
    l_down = load(Q + 2, w_down, vw_down)
    l_out = load(Q + 3, w_out, vw_out)
    l_proj = load(Q + 4, proj, vproj)
    l_resid = load(Q + 5, resid, vresid)
    l_stud = load(Q + 6, stud, vstud)
    for cp in [l_gate, l_up, l_down, l_out] + own_a + [l_proj, l_resid, l_stud]:
        cp.start()

    out_copies = [
        load(Q + 7, gate_grad, gate_out), load(Q + 8, up_grad, up_out), load(Q + 9, down_grad, down_out),
    ]

    barrier = pltpu.get_barrier_semaphore()
    for peer in [sib, far, yn, yp] + xs + xo + zs:
        pl.semaphore_signal(barrier, 1, device_id=peer, device_id_type=MESH)
    for k in range(4):

        @pl.when(other[k])
        def _():
            pl.semaphore_signal(barrier, 1, device_id=mirror_from[k], device_id_type=MESH)

    pl.semaphore_wait(barrier, jnp.where(d != t, 17, 16))

    started = []

    def send(slot, src, dst, peer):
        cp = pltpu.make_async_remote_copy(
            src, dst, ss.at[slot], rs.at[slot], device_id=peer, device_id_type=MESH
        )
        cp.start()
        started.append(cp)
        return cp

    def gather_dp_own(base, own, place, place2):
        dst = place(x, zh, c)
        m = {}
        m["z"] = send(base, own, dst, far)
        for k in (1, 2, 3):
            m["x", k] = send(base + k, own, dst, xs[k - 1])
        m["s0"] = send(base + 4, own, dst, sib)
        return m

    def gather_dp_far(base, m, place, place2):
        m["z"].wait_recv()
        piece = place(x, 1 - zh, c)
        for k in (1, 2, 3):
            m["zx", k] = send(base + 4 + k, piece, piece, xs[k - 1])
        m["s1"] = send(base + 8, piece, piece, sib)

    def gather_dp_sib(base, m, place, place2):
        for k in (1, 3, 2):
            m["x", k].wait_recv()
            m["zx", k].wait_recv()
            piece = place2(ring(x, 4 - k), c)
            m["s", k] = send(base + 8 + k, piece, piece, sib)

    def gather_dp_end(m):
        m["s0"].wait_recv()
        m["s1"].wait_recv()
        for k in (1, 3, 2):
            m["s", k].wait_recv()

    def scatter_y_first(base, part, a1):
        far_y = ring(y, 2)
        m = {}
        m["h0"] = send(base, part.at[far_y, pl.ds(0, 2)], a1.at[0], yn)
        m["h1"] = send(base + 1, part.at[far_y, pl.ds(2, 2)], a1.at[1], yp)
        return m

    def scatter_y_raw(base, m, part, a2):
        m["r0"] = send(base + 2, part.at[ring(y, 1), pl.ds(2, 2)], a2.at[0, pl.ds(2, 2)], yn)
        m["r1"] = send(base + 3, part.at[ring(y, 3), pl.ds(0, 2)], a2.at[1, pl.ds(0, 2)], yp)

    def scatter_y_forward(base, m, part, a1, a2):
        for side, (lo, to, peer) in enumerate(((0, ring(y, 1), yn), (2, ring(y, 3), yp))):
            m["h%d" % side].wait_recv()
            for i in range(2):
                both = part[to, lo + i].astype(F32) + a1[side, i].astype(F32)
                part[to, lo + i] = both.astype(BF16)
            m["c%d" % side] = send(
                base + 4 + side, part.at[to, pl.ds(lo, 2)], a2.at[side, pl.ds(lo, 2)], peer
            )

    def scatter_z(base, m, part, a2, res, az):
        for n in ("r0", "r1", "c0", "c1"):
            m[n].wait_recv()
        for i in range(4):
            total = part[y, i].astype(F32) + a2[0, i].astype(F32) + a2[1, i].astype(F32)
            res[i] = total.astype(BF16)
        for k in (1, 2, 3):
            m["z", k] = send(base + 5 + k, res.at[ring(zl, k)], az.at[k - 1], zs[k - 1])

    def scatter_end(m, res, az):
        for k in (1, 2, 3):
            m["z", k].wait_recv()
        total = res[zl].astype(F32)
        for k in range(3):
            total += az[k].astype(F32)
        return total

    def gather_z(base, view, early=False):
        own = view(y, zl, 1)
        m = {("z", k): send(base + k - 1, own, own, zs[k - 1]) for k in (1, 2, 3)}
        m["early"] = early
        if early:
            m["y0", 0] = send(base + 3, own, own, yn)
            m["y1", 0] = send(base + 4, own, own, yp)
        return m

    def gather_y(base, m, view):
        if m["early"]:
            for k in (1, 3, 2):
                m["z", k].wait_recv()
                piece = view(y, ring(zl, 4 - k), 1)
                m["y0", k] = send(base + 3 + 2 * k, piece, piece, yn)
                m["y1", k] = send(base + 4 + 2 * k, piece, piece, yp)
        else:
            for k in (1, 2, 3):
                if ("z", k) in m:
                    m["z", k].wait_recv()
            mine = view(y, 0, 4)
            m["y0", 0] = send(base + 3, mine, mine, yn)
            m["y1", 0] = send(base + 4, mine, mine, yp)

    def gather_forward(base, m, view):
        base += 11 if m["early"] else 5
        for side, (far_y, lo, peer) in enumerate(((ring(y, 3), 0, yn), (ring(y, 1), 2, yp))):
            for k in (0, 1, 3, 2) if m["early"] else (0,):
                m["y%d" % side, k].wait_recv()
            half = view(far_y, lo, 2)
            m["f%d" % side] = send(base + side, half, half, peer)

    def gather_end(m):
        m["f0"].wait_recv()
        m["f1"].wait_recv()

    A = [None] * Q
    B = [None] * Q
    C = [None] * Q
    D = [{} for _ in range(Q)]
    E = [None] * Q
    EM = [None] * Q

    def g_place(q):
        return lambda x_, zh_, c_: g.at[q, x_, zh_, c_]

    def g_place2(q):
        return lambda x_, c_: g.at[q, x_, :, c_]

    def ta_view(q):
        return lambda y_, lo, n: ta.at[q, y_, pl.ds(lo, n)]

    def ma_view(q):
        def view(y_, lo, n):
            start = pl.multiple_of((y_ * 4 + lo) * DC, DC)
            return ma.at[pl.ds(q * S, S), pl.ds(start, n * DC)]

        return view

    def mb_view(q):
        rows = pl.ds(q * S, S)

        def view(y_, lo, n):
            if n == 1:
                return mb.at[lax.rem(lo, 2), y_ * 2 + lo // 2, rows]
            if n == 2:
                return mb.at[:, y_ * 2 + lo // 2, rows]
            return mb.at[:, pl.ds(y_ * 2, 2), rows]

        return view

    def mix(q):
        def cols(n, _):
            at = pl.ds(pl.multiple_of(n * 256, 256), 256)
            out = jnp.dot(g[q].reshape(16 * S, DK), vw_out[:, at], preferred_element_type=F32)
            p1[q, :, :, :, at] = out.astype(BF16).reshape(4, 4, S, 256)
            return 0

        lax.fori_loop(0, DK // 256, cols, 0)

    def map_target(q, yg):
        out = jnp.dot(ta[q, yg].reshape(4 * S, DK), vproj[...], preferred_element_type=F32)
        p2[q, yg] = out.astype(BF16).reshape(2, 2, S, DC)

    def s_far(q):
        gather_dp_far(A0 + A_SLOTS * q, A[q], g_place(q), g_place2(q))

    def s_sib(q):
        gather_dp_sib(A0 + A_SLOTS * q, A[q], g_place(q), g_place2(q))

    def s_own(q):
        base = A0 + A_SLOTS * q
        A[q] = gather_dp_own(base, attn.at[pl.ds(q * S, S)], g_place(q), g_place2(q))

    def s_mix(q):
        own_a[q].wait()
        gather_dp_end(A[q])
        mix(q)
        B[q] = scatter_y_first(B0 + B_SLOTS * q, p1.at[q], y1.at[q])
        scatter_y_raw(B0 + B_SLOTS * q, B[q], p1.at[q], y2.at[q])

    def s_forward(q):
        scatter_y_forward(B0 + B_SLOTS * q, B[q], p1.at[q], y1.at[q], y2.at[q])

    def s_z(q):
        scatter_z(B0 + B_SLOTS * q, B[q], p1.at[q], y2.at[q], r.at[q], zr.at[q])

    def s_state(q):
        total = scatter_end(B[q], r.at[q], zr.at[q])
        state = total + vresid[pl.ds(q * S, S)].astype(F32)
        ta[q, y, zl] = state.astype(BF16)
        C[q] = gather_z(C0 + C_SLOTS * q, ta_view(q), early=True)

    def s_all_y(q):
        gather_y(C0 + C_SLOTS * q, C[q], ta_view(q))

    def s_all_forward(q):
        gather_forward(C0 + C_SLOTS * q, C[q], ta_view(q))

    def s_map(q):
        map_target(q, y)
        map_target(q, ring(y, 1))
        map_target(q, ring(y, 3))

    def s_target(q):
        gather_end(C[q])
        map_target(q, ring(y, 2))
        base = D0 + D_SLOTS * q
        for k in (1, 3, 2):
            D[q][k - 1] = send(base + k - 1, p2.at[q, ring(x, k), :, c], dx.at[q, k - 1], xs[k - 1])
            D[q][k + 2] = send(base + k + 2, p2.at[q, ring(x, k), :, 1 - c], dx.at[q, k + 2], xo[k - 1])
        D[q][6] = send(base + 6, p2.at[q, x, :, 1 - c], dx.at[q, 6], sib)

    def s_target_z(q):
        for k in range(7):
            D[q][k].wait_recv()
        total = p2[q, x, :, c].astype(F32)
        for k in range(7):
            total += dx[q, k].astype(F32)
        p4[q] = total
        p4b[q] = total.astype(BF16)
        D[q]["z"] = send(D0 + D_SLOTS * q + 7, p4b.at[q, 1 - zh], dz.at[q], far)

    def s_mismatch(q):
        D[q]["z"].wait_recv()
        rows = pl.ds(q * S, S)
        target = p4[q, zh] + dz[q].astype(F32)
        diff = (vstud[rows].astype(F32) + so[rows] - target).astype(BF16)
        mt[q] = diff
        col = pl.multiple_of(t * DC, DC)
        ma[rows, pl.ds(col, DC)] = diff
        base = E0 + E_SLOTS * q
        for k in range(4):

            @pl.when(other[k])
            def _():
                mirror_copy(q, k, lax.rem(d, 4), d).start()

        @pl.when(d == t)
        def _():
            mb[lax.rem(d, 2), d // 2, rows] = diff

        E[q] = gather_z(base, ma_view(q))

    def mirror_copy(q, k, slot, owner):
        base = E0 + E_SLOTS * q + E_MIRROR
        return pltpu.make_async_remote_copy(
            mt.at[q], mb.at[lax.rem(owner, 2), owner // 2, pl.ds(q * S, S)],
            ss.at[base + k], rs.at[base + slot],
            device_id=mirror_to[k], device_id_type=MESH,
        )

    def s_ey(q):
        gather_y(E0 + E_SLOTS * q, E[q], ma_view(q))

    def s_fy(q):
        for k in range(4):

            @pl.when(other[k])
            def _():
                mirror_copy(q, k, k, (t // 4) * 4 + k).wait_recv()

        EM[q] = {"early": False}
        gather_y(E0 + E_SLOTS * q + E_GATHER, EM[q], mb_view(q))

    def s_ef(q):
        gather_forward(E0 + E_SLOTS * q, E[q], ma_view(q))

    def s_ff(q):
        gather_forward(E0 + E_SLOTS * q + E_GATHER, EM[q], mb_view(q))
        for k in range(4):

            @pl.when(other[k])
            def _():
                mirror_copy(q, k, k, d).wait_send()

    def s_ee(q):
        gather_end(E[q])

    def s_fe(q):
        gather_end(EM[q])

    st = {}

    def ht_place(x_, zh_, c_):
        return ht.at[c_, :, pl.ds(pl.multiple_of((x_ * 2 + zh_) * TOK, TOK), TOK)]

    def ht_place2(x_, c_):
        return ht.at[c_, :, pl.ds(pl.multiple_of(x_ * 2 * TOK, 2 * TOK), 2 * TOK)]

    def hide():
        l_gate.wait()
        l_up.wait()
        gf = vgate[...].astype(F32)
        h = (gf * jax.nn.sigmoid(gf) * vup[...].astype(F32)).astype(BF16)
        hid[...] = h
        ht[c, :, pl.ds(pl.multiple_of((x * 2 + zh) * TOK, TOK), TOK)] = h.astype(F32).T.astype(BF16)

    def student_part(first, last):
        def cols(i, _):
            at = pl.ds(pl.multiple_of(i * DC, DC), DC)
            out = jnp.dot(hid[...], vw_down[:, at], preferred_element_type=F32)
            sp[i // 4, lax.rem(i, 4)] = out.astype(BF16)
            return 0

        lax.fori_loop(first, last, cols, 0)

    def student_a():
        l_down.wait()
        student_part(0, 8)

    def student():
        student_part(8, 16)
        st["m"] = scatter_y_first(SB0, sp, sy1)
        scatter_y_raw(SB0, st["m"], sp, sy2)

    def student_forward():
        scatter_y_forward(SB0, st["m"], sp, sy1, sy2)

    def student_z():
        scatter_z(SB0, st["m"], sp, sy2, sr, szr)

    def student_end():
        so[...] = scatter_end(st["m"], sr, szr)

    def hidden_own():
        st["h"] = gather_dp_own(H0, ht_place(x, zh, c), ht_place, ht_place2)

    def hidden_far():
        gather_dp_far(H0, st["h"], ht_place, ht_place2)

    def hidden_end():
        gather_dp_end(st["h"])

    def hidden_sib():
        gather_dp_sib(H0, st["h"], ht_place, ht_place2)

    def turn():
        def block(i, _):
            at = pl.ds(pl.multiple_of(i * 128, 128), 128)
            vturned[at, :] = vw_down[:, at].T
            return 0

        lax.fori_loop(0, DS // 128, block, 0)

    def gate_up():
        def cols(i, _):
            at = pl.ds(pl.multiple_of(i * 128, 128), 128)
            hg = jnp.dot(ma[...], vturned[:, at], preferred_element_type=F32)
            gf = vgate[:, at].astype(F32)
            uf = vup[:, at].astype(F32)
            sg = jax.nn.sigmoid(gf)
            gate_grad[:, at] = hg * uf * sg * (1.0 + gf * (1.0 - sg))
            up_grad[:, at] = hg * gf * sg
            return 0

        lax.fori_loop(0, FF // 128, cols, 0)
        for cp in out_copies[:2]:
            cp.start()

    def down():
        def block(i, _):
            at = pl.ds(pl.multiple_of(i * 448, 64), 448)
            out = jnp.dot(ht[0, at], mb[0].reshape(8 * TOK, DC), preferred_element_type=F32)
            out += jnp.dot(ht[1, at], mb[1].reshape(8 * TOK, DC), preferred_element_type=F32)
            down_grad[at] = out
            return 0

        lax.fori_loop(0, FF // 448, block, 0)
        out_copies[2].start()

    waited = set()

    def once(cp):
        if id(cp) not in waited:
            waited.add(id(cp))
            cp.wait()

    steps = {
        "own": s_own, "far": s_far, "sib": s_sib, "mix": s_mix, "fwd": s_forward,
        "z": s_z, "state": s_state, "ally": s_all_y, "allf": s_all_forward, "map": s_map,
        "tgt": s_target, "tz": s_target_z, "mis": s_mismatch,
        "ey": s_ey, "fy": s_fy, "ef": s_ef, "ff": s_ff, "ee": s_ee, "fe": s_fe,
        "hide": hide, "sta": student_a, "student": student, "stf": student_forward, "stz": student_z, "ste": student_end,
        "hown": hidden_own, "hfar": hidden_far, "hsib": hidden_sib, "hend": hidden_end,
        "turn": turn, "grads": gate_up, "down": down,
    }
    before = {"mix": l_out, "state": l_resid, "map": l_proj, "mis": l_stud}
    for step in ORDER:
        name, _, q = step.partition(".")
        if name in before:
            once(before[name])
        if q:
            steps[name](int(q))
        else:
            steps[name]()
        while len(started) > IN_FLIGHT:
            started.pop(0).wait_send()
    for cp in started:
        cp.wait_send()
    for cp in out_copies:
        cp.wait()


def hand_out(a, b, c, a_out, b_out, c_out, a_held, b_held, c_held, sem):
    held = (a_held, b_held, c_held)
    ins = [pltpu.make_async_copy(src, v, sem.at[i]) for i, (src, v) in enumerate(zip((a, b, c), held))]
    outs = [
        pltpu.make_async_copy(v, dst, sem.at[3 + i])
        for i, (v, dst) in enumerate(zip(held, (a_out, b_out, c_out)))
    ]
    for cp in ins:
        cp.start()
    for first, then in zip(ins, outs):
        first.wait()
        then.start()
    for cp in outs:
        cp.wait()


def per_device(attn_out, teacher_resid, w_out, projection, student_in, gate_act, up_act, w_down):
    def vmem(*shape, dtype=BF16):
        return pltpu.VMEM(shape, dtype)

    grads = pl.pallas_call(
        kernel,
        out_shape=(
            jax.ShapeDtypeStruct((TOK, FF), F32),
            jax.ShapeDtypeStruct((TOK, FF), F32),
            jax.ShapeDtypeStruct((FF, DC), F32),
        ),
        in_specs=[pl.BlockSpec(memory_space=pl.ANY)] * 8,
        out_specs=(pl.BlockSpec(memory_space=pl.ANY),) * 3,
        scratch_shapes=[
            vmem(TOK, FF, dtype=F32),
            vmem(TOK, FF, dtype=F32),
            vmem(FF, DC, dtype=F32),
            vmem(Q, 4, 2, 2, S, DK),
            vmem(Q, 4, 4, S, DK),
            vmem(Q, 2, 2, S, DK),
            vmem(Q, 2, 4, S, DK),
            vmem(Q, 4, S, DK),
            vmem(Q, 3, S, DK),
            vmem(Q, 4, 4, S, DK),
            vmem(Q, 4, 2, 2, S, DC),
            vmem(Q, 7, 2, S, DC),
            vmem(Q, 2, S, DC, dtype=F32),
            vmem(Q, 2, S, DC),
            vmem(Q, S, DC),
            vmem(TOK, DS),
            vmem(Q, S, DC),
            vmem(2, 8, TOK, DC),
            vmem(TOK, FF),
            vmem(2, FF, 8 * TOK),
            vmem(4, 4, TOK, DC),
            vmem(2, 2, TOK, DC),
            vmem(2, 4, TOK, DC),
            vmem(4, TOK, DC),
            vmem(3, TOK, DC),
            vmem(TOK, DC, dtype=F32),
            vmem(DK, DK),
            vmem(DK, DC),
            vmem(FF, DS),
            vmem(DS, FF),
            vmem(TOK, DK),
            vmem(TOK, DC),
            vmem(TOK, FF),
            vmem(TOK, FF),
            pltpu.SemaphoreType.DMA((N_SLOTS,)),
            pltpu.SemaphoreType.DMA((N_SLOTS,)),
            pltpu.SemaphoreType.DMA((Q + 10,)),
        ],
        compiler_params=pltpu.CompilerParams(
            collective_id=0, has_side_effects=True, vmem_limit_bytes=58 * 2**20
        ),
        name="distill_step",
    )(attn_out, teacher_resid, w_out, projection, student_in, gate_act, up_act, w_down)
    return pl.pallas_call(
        hand_out,
        out_shape=tuple(jax.ShapeDtypeStruct(g.shape, g.dtype) for g in grads),
        in_specs=[pl.BlockSpec(memory_space=pl.ANY)] * 3,
        out_specs=(pl.BlockSpec(memory_space=pl.ANY),) * 3,
        scratch_shapes=[pltpu.VMEM(g.shape, g.dtype) for g in grads] + [pltpu.SemaphoreType.DMA((6,))],
        name="hand_out",
    )(*grads)


def solution(mesh):
    in_specs = (
        P("dp", "tensor"),
        P("tensor", "dp"),
        P("tensor", "dp"),
        P("dp", "tensor"),
        P("dp", "tensor"),
        P("dp", "tensor"),
        P("dp", "tensor"),
        P("tensor", None),
    )
    out_specs = (P("dp", "tensor"), P("dp", "tensor"), P("tensor", "dp"))
    return jax.shard_map(
        per_device, mesh=mesh, in_specs=in_specs, out_specs=out_specs, check_vma=False
    )
```

```python
import functools

import jax
import jax.numpy as jnp
from jax import lax
from jax.experimental import pallas as pl
from jax.experimental.pallas import tpu as pltpu
from jax.sharding import PartitionSpec as P

MESH = pl.DeviceIdType.MESH
F32 = jnp.float32
BF16 = jnp.bfloat16

Q = 4
TOK = 128
S = TOK // Q
DK = 1024
DC = 256
DS = 4096
FF = 896
ORDER = ("own.0", "hide", "sta", "far.0", "own.1", "own.2", "student", "sib.0", "far.1", "own.3", "mix.0", "sib.1", "far.2", "far.3", "hown", "fwd.0", "mix.1", "z.0", "sib.3", "fwd.1", "mix.3", "z.1", "hfar", "sib.2", "state.0", "fwd.3", "mix.2", "state.1", "fwd.2", "z.3", "stf", "ally.0", "z.2", "ally.1", "turn", "state.3", "allf.0", "allf.1", "state.2", "map.1", "hsib", "map.0", "tgt.0", "ally.3", "tgt.1", "stz", "ally.2", "tz.0", "allf.3", "tz.1", "ste", "allf.2", "mis.1", "map.2", "map.3", "tgt.3", "mis.0", "tgt.2", "hend", "ey.1", "fy.1", "ey.0", "tz.3", "fy.0", "ef.1", "tz.2", "ff.1", "mis.3", "ef.0", "ff.0", "fe.1", "mis.2", "ey.3", "fy.3", "ey.2", "fe.0", "fy.2", "ee.1", "ff.3", "ef.3", "ef.2", "ff.2", "grada", "downa", "ee.3", "fe.3", "ee.0", "ee.2", "grads", "fe.2", "down")

A_SLOTS, B_SLOTS, C_SLOTS, D_SLOTS, E_SLOTS = 12, 9, 13, 8, 15
E_GATHER = 4
E_MIRROR = 11
IN_FLIGHT = 60
A0 = 0
B0 = A0 + A_SLOTS * Q
C0 = B0 + B_SLOTS * Q
D0 = C0 + C_SLOTS * Q
E0 = D0 + D_SLOTS * Q
SB0 = E0 + E_SLOTS * Q
H0 = SB0 + B_SLOTS
N_SLOTS = H0 + A_SLOTS


def kernel(
    attn, resid, w_out, proj, stud, gate, up, w_down,
    gate_out, up_out, down_out,
    gate_grad, up_grad, down_grad, g, p1, y1, y2, r, zr, ta, p2, dx, p4, p4b, dz,
    ma, mt, mb, hid, ht, sp, sy1, sy2, sr, szr, so,
    vw_out, vproj, vw_down, vturned, vresid, vstud, vgate, vup,
    ss, rs, ls,
):
    d = lax.axis_index("dp")
    t = lax.axis_index("tensor")
    x, zh, c = d // 4, lax.rem(d // 2, 2), lax.rem(d, 2)
    y, zl = t // 4, lax.rem(t, 4)

    def dev(x_, zh_, c_, y_, zl_):
        return ((x_ * 2 + zh_) * 2 + c_, y_ * 4 + zl_)

    def ring(a, k):
        return lax.rem(a + k, 4)

    sib = dev(x, zh, 1 - c, y, zl)
    far = dev(x, 1 - zh, c, y, zl)
    xs = [dev(ring(x, k), zh, c, y, zl) for k in (1, 2, 3)]
    zs = [dev(x, zh, c, y, ring(zl, k)) for k in (1, 2, 3)]
    yn, yp = dev(x, zh, c, ring(y, 1), zl), dev(x, zh, c, ring(y, 3), zl)
    xo = [dev(ring(x, k), zh, 1 - c, y, zl) for k in (1, 2, 3)]
    mirror_to = [(t, (d // 4) * 4 + k) for k in range(4)]
    mirror_from = [((t // 4) * 4 + k, d) for k in range(4)]
    other = [jnp.logical_or(d != t, lax.rem(d, 4) != k) for k in range(4)]

    def load(i, src, dst):
        return pltpu.make_async_copy(src, dst, ls.at[i])

    own_a = [load(q, attn.at[pl.ds(q * S, S)], g.at[q, x, zh, c]) for q in range(Q)]
    l_gate = load(Q, gate, vgate)
    l_up = load(Q + 1, up, vup)
    l_down = load(Q + 2, w_down, vw_down)
    l_out = load(Q + 3, w_out, vw_out)
    l_proj = load(Q + 4, proj, vproj)
    l_resid = load(Q + 5, resid, vresid)
    l_stud = load(Q + 6, stud, vstud)
    for cp in [l_gate, l_up, l_down, l_out] + own_a + [l_proj, l_resid, l_stud]:
        cp.start()

    out_copies = [
        load(Q + 7, gate_grad, gate_out), load(Q + 8, up_grad, up_out), load(Q + 9, down_grad, down_out),
    ]

    barrier = pltpu.get_barrier_semaphore()
    for peer in [sib, far, yn, yp] + xs + xo + zs:
        pl.semaphore_signal(barrier, 1, device_id=peer, device_id_type=MESH)
    for k in range(4):

        @pl.when(other[k])
        def _():
            pl.semaphore_signal(barrier, 1, device_id=mirror_from[k], device_id_type=MESH)

    pl.semaphore_wait(barrier, jnp.where(d != t, 17, 16))

    started = []

    def send(slot, src, dst, peer):
        cp = pltpu.make_async_remote_copy(
            src, dst, ss.at[slot], rs.at[slot], device_id=peer, device_id_type=MESH
        )
        cp.start()
        started.append(cp)
        return cp

    def gather_dp_own(base, own, place, place2):
        dst = place(x, zh, c)
        m = {}
        m["z"] = send(base, own, dst, far)
        for k in (1, 2, 3):
            m["x", k] = send(base + k, own, dst, xs[k - 1])
        m["s0"] = send(base + 4, own, dst, sib)
        return m

    def gather_dp_far(base, m, place, place2):
        m["z"].wait_recv()
        piece = place(x, 1 - zh, c)
        for k in (1, 2, 3):
            m["zx", k] = send(base + 4 + k, piece, piece, xs[k - 1])
        m["s1"] = send(base + 8, piece, piece, sib)

    def gather_dp_sib(base, m, place, place2):
        for k in (1, 3, 2):
            m["x", k].wait_recv()
            m["zx", k].wait_recv()
            piece = place2(ring(x, 4 - k), c)
            m["s", k] = send(base + 8 + k, piece, piece, sib)

    def gather_dp_end(m):
        m["s0"].wait_recv()
        m["s1"].wait_recv()
        for k in (1, 3, 2):
            m["s", k].wait_recv()

    def scatter_y_first(base, part, a1):
        far_y = ring(y, 2)
        m = {}
        m["h0"] = send(base, part.at[far_y, pl.ds(0, 2)], a1.at[0], yn)
        m["h1"] = send(base + 1, part.at[far_y, pl.ds(2, 2)], a1.at[1], yp)
        return m

    def scatter_y_raw(base, m, part, a2):
        m["r0"] = send(base + 2, part.at[ring(y, 1), pl.ds(2, 2)], a2.at[0, pl.ds(2, 2)], yn)
        m["r1"] = send(base + 3, part.at[ring(y, 3), pl.ds(0, 2)], a2.at[1, pl.ds(0, 2)], yp)

    def scatter_y_forward(base, m, part, a1, a2):
        for side, (lo, to, peer) in enumerate(((0, ring(y, 1), yn), (2, ring(y, 3), yp))):
            m["h%d" % side].wait_recv()
            for i in range(2):
                both = part[to, lo + i].astype(F32) + a1[side, i].astype(F32)
                part[to, lo + i] = both.astype(BF16)
            m["c%d" % side] = send(
                base + 4 + side, part.at[to, pl.ds(lo, 2)], a2.at[side, pl.ds(lo, 2)], peer
            )

    def scatter_z(base, m, part, a2, res, az):
        for n in ("r0", "r1", "c0", "c1"):
            m[n].wait_recv()
        for i in range(4):
            total = part[y, i].astype(F32) + a2[0, i].astype(F32) + a2[1, i].astype(F32)
            res[i] = total.astype(BF16)
        for k in (1, 2, 3):
            m["z", k] = send(base + 5 + k, res.at[ring(zl, k)], az.at[k - 1], zs[k - 1])

    def scatter_end(m, res, az):
        for k in (1, 2, 3):
            m["z", k].wait_recv()
        total = res[zl].astype(F32)
        for k in range(3):
            total += az[k].astype(F32)
        return total

    def gather_z(base, view, early=False):
        own = view(y, zl, 1)
        m = {("z", k): send(base + k - 1, own, own, zs[k - 1]) for k in (1, 2, 3)}
        m["early"] = early
        if early:
            m["y0", 0] = send(base + 3, own, own, yn)
            m["y1", 0] = send(base + 4, own, own, yp)
        return m

    def gather_y(base, m, view):
        if m["early"]:
            for k in (1, 3, 2):
                m["z", k].wait_recv()
                piece = view(y, ring(zl, 4 - k), 1)
                m["y0", k] = send(base + 3 + 2 * k, piece, piece, yn)
                m["y1", k] = send(base + 4 + 2 * k, piece, piece, yp)
        else:
            for k in (1, 2, 3):
                if ("z", k) in m:
                    m["z", k].wait_recv()
            mine = view(y, 0, 4)
            m["y0", 0] = send(base + 3, mine, mine, yn)
            m["y1", 0] = send(base + 4, mine, mine, yp)

    def gather_forward(base, m, view):
        base += 11 if m["early"] else 5
        for side, (far_y, lo, peer) in enumerate(((ring(y, 3), 0, yn), (ring(y, 1), 2, yp))):
            for k in (0, 1, 3, 2) if m["early"] else (0,):
                m["y%d" % side, k].wait_recv()
            half = view(far_y, lo, 2)
            m["f%d" % side] = send(base + side, half, half, peer)

    def gather_end(m):
        m["f0"].wait_recv()
        m["f1"].wait_recv()

    A = [None] * Q
    B = [None] * Q
    C = [None] * Q
    D = [{} for _ in range(Q)]
    E = [None] * Q
    EM = [None] * Q

    def g_place(q):
        return lambda x_, zh_, c_: g.at[q, x_, zh_, c_]

    def g_place2(q):
        return lambda x_, c_: g.at[q, x_, :, c_]

    def ta_view(q):
        return lambda y_, lo, n: ta.at[q, y_, pl.ds(lo, n)]

    def ma_view(q):
        def view(y_, lo, n):
            start = pl.multiple_of((y_ * 4 + lo) * DC, DC)
            return ma.at[pl.ds(q * S, S), pl.ds(start, n * DC)]

        return view

    def mb_view(q):
        rows = pl.ds(q * S, S)

        def view(y_, lo, n):
            if n == 1:
                return mb.at[lax.rem(lo, 2), y_ * 2 + lo // 2, rows]
            if n == 2:
                return mb.at[:, y_ * 2 + lo // 2, rows]
            return mb.at[:, pl.ds(y_ * 2, 2), rows]

        return view

    def mix(q):
        def cols(n, _):
            at = pl.ds(pl.multiple_of(n * 256, 256), 256)
            out = jnp.dot(g[q].reshape(16 * S, DK), vw_out[:, at], preferred_element_type=F32)
            p1[q, :, :, :, at] = out.astype(BF16).reshape(4, 4, S, 256)
            return 0

        lax.fori_loop(0, DK // 256, cols, 0)

    def map_target(q, yg):
        out = jnp.dot(ta[q, yg].reshape(4 * S, DK), vproj[...], preferred_element_type=F32)
        p2[q, yg] = out.astype(BF16).reshape(2, 2, S, DC)

    def s_far(q):
        gather_dp_far(A0 + A_SLOTS * q, A[q], g_place(q), g_place2(q))

    def s_sib(q):
        gather_dp_sib(A0 + A_SLOTS * q, A[q], g_place(q), g_place2(q))

    def s_own(q):
        base = A0 + A_SLOTS * q
        A[q] = gather_dp_own(base, attn.at[pl.ds(q * S, S)], g_place(q), g_place2(q))

    def s_mix(q):
        own_a[q].wait()
        gather_dp_end(A[q])
        mix(q)
        B[q] = scatter_y_first(B0 + B_SLOTS * q, p1.at[q], y1.at[q])
        scatter_y_raw(B0 + B_SLOTS * q, B[q], p1.at[q], y2.at[q])

    def s_forward(q):
        scatter_y_forward(B0 + B_SLOTS * q, B[q], p1.at[q], y1.at[q], y2.at[q])

    def s_z(q):
        scatter_z(B0 + B_SLOTS * q, B[q], p1.at[q], y2.at[q], r.at[q], zr.at[q])

    def s_state(q):
        total = scatter_end(B[q], r.at[q], zr.at[q])
        state = total + vresid[pl.ds(q * S, S)].astype(F32)
        ta[q, y, zl] = state.astype(BF16)
        C[q] = gather_z(C0 + C_SLOTS * q, ta_view(q), early=True)

    def s_all_y(q):
        gather_y(C0 + C_SLOTS * q, C[q], ta_view(q))

    def s_all_forward(q):
        gather_forward(C0 + C_SLOTS * q, C[q], ta_view(q))

    def s_map(q):
        map_target(q, y)
        map_target(q, ring(y, 1))
        map_target(q, ring(y, 3))

    def s_target(q):
        gather_end(C[q])
        map_target(q, ring(y, 2))
        base = D0 + D_SLOTS * q
        for k in (1, 3, 2):
            D[q][k - 1] = send(base + k - 1, p2.at[q, ring(x, k), :, c], dx.at[q, k - 1], xs[k - 1])
            D[q][k + 2] = send(base + k + 2, p2.at[q, ring(x, k), :, 1 - c], dx.at[q, k + 2], xo[k - 1])
        D[q][6] = send(base + 6, p2.at[q, x, :, 1 - c], dx.at[q, 6], sib)

    def s_target_z(q):
        for k in range(7):
            D[q][k].wait_recv()
        total = p2[q, x, :, c].astype(F32)
        for k in range(7):
            total += dx[q, k].astype(F32)
        p4[q] = total
        p4b[q] = total.astype(BF16)
        D[q]["z"] = send(D0 + D_SLOTS * q + 7, p4b.at[q, 1 - zh], dz.at[q], far)

    def s_mismatch(q):
        D[q]["z"].wait_recv()
        rows = pl.ds(q * S, S)
        target = p4[q, zh] + dz[q].astype(F32)
        diff = (vstud[rows].astype(F32) + so[rows] - target).astype(BF16)
        mt[q] = diff
        col = pl.multiple_of(t * DC, DC)
        ma[rows, pl.ds(col, DC)] = diff
        base = E0 + E_SLOTS * q
        for k in range(4):

            @pl.when(other[k])
            def _():
                mirror_copy(q, k, lax.rem(d, 4), d).start()

        @pl.when(d == t)
        def _():
            mb[lax.rem(d, 2), d // 2, rows] = diff

        E[q] = gather_z(base, ma_view(q))

    def mirror_copy(q, k, slot, owner):
        base = E0 + E_SLOTS * q + E_MIRROR
        return pltpu.make_async_remote_copy(
            mt.at[q], mb.at[lax.rem(owner, 2), owner // 2, pl.ds(q * S, S)],
            ss.at[base + k], rs.at[base + slot],
            device_id=mirror_to[k], device_id_type=MESH,
        )

    def s_ey(q):
        gather_y(E0 + E_SLOTS * q, E[q], ma_view(q))

    def s_fy(q):
        for k in range(4):

            @pl.when(other[k])
            def _():
                mirror_copy(q, k, k, (t // 4) * 4 + k).wait_recv()

        EM[q] = {"early": False}
        gather_y(E0 + E_SLOTS * q + E_GATHER, EM[q], mb_view(q))

    def s_ef(q):
        gather_forward(E0 + E_SLOTS * q, E[q], ma_view(q))

    def s_ff(q):
        gather_forward(E0 + E_SLOTS * q + E_GATHER, EM[q], mb_view(q))
        for k in range(4):

            @pl.when(other[k])
            def _():
                mirror_copy(q, k, k, d).wait_send()

    def s_ee(q):
        gather_end(E[q])

    def s_fe(q):
        gather_end(EM[q])

    st = {}

    def ht_place(x_, zh_, c_):
        return ht.at[c_, :, pl.ds(pl.multiple_of((x_ * 2 + zh_) * TOK, TOK), TOK)]

    def ht_place2(x_, c_):
        return ht.at[c_, :, pl.ds(pl.multiple_of(x_ * 2 * TOK, 2 * TOK), 2 * TOK)]

    def hide():
        l_gate.wait()
        l_up.wait()
        gf = vgate[...].astype(F32)
        h = (gf * jax.nn.sigmoid(gf) * vup[...].astype(F32)).astype(BF16)
        hid[...] = h
        ht[c, :, pl.ds(pl.multiple_of((x * 2 + zh) * TOK, TOK), TOK)] = h.astype(F32).T.astype(BF16)

    def student_part(first, last):
        def cols(i, _):
            at = pl.ds(pl.multiple_of(i * DC, DC), DC)
            out = jnp.dot(hid[...], vw_down[:, at], preferred_element_type=F32)
            sp[i // 4, lax.rem(i, 4)] = out.astype(BF16)
            return 0

        lax.fori_loop(first, last, cols, 0)

    def student_a():
        l_down.wait()
        student_part(0, 8)

    def student():
        student_part(8, 16)
        st["m"] = scatter_y_first(SB0, sp, sy1)
        scatter_y_raw(SB0, st["m"], sp, sy2)

    def student_forward():
        scatter_y_forward(SB0, st["m"], sp, sy1, sy2)

    def student_z():
        scatter_z(SB0, st["m"], sp, sy2, sr, szr)

    def student_end():
        so[...] = scatter_end(st["m"], sr, szr)

    def hidden_own():
        st["h"] = gather_dp_own(H0, ht_place(x, zh, c), ht_place, ht_place2)

    def hidden_far():
        gather_dp_far(H0, st["h"], ht_place, ht_place2)

    def hidden_end():
        gather_dp_end(st["h"])

    def hidden_sib():
        gather_dp_sib(H0, st["h"], ht_place, ht_place2)

    def turn():
        def block(i, _):
            at = pl.ds(pl.multiple_of(i * 128, 128), 128)
            vturned[at, :] = vw_down[:, at].T
            return 0

        lax.fori_loop(0, DS // 128, block, 0)

    def hidden_part(at, y_):
        k = pl.ds(pl.multiple_of(y_ * 4 * DC, 4 * DC), 4 * DC)
        return jnp.dot(ma[:, k], vturned[k, at], preferred_element_type=F32)

    def gate_up_near():
        def cols(i, _):
            at = pl.ds(pl.multiple_of(i * 128, 128), 128)
            near = hidden_part(at, y) + hidden_part(at, ring(y, 1)) + hidden_part(at, ring(y, 3))
            gate_grad[:, at] = near
            return 0

        lax.fori_loop(0, FF // 128, cols, 0)

    def gate_up():
        def cols(i, _):
            at = pl.ds(pl.multiple_of(i * 128, 128), 128)
            hg = gate_grad[:, at] + hidden_part(at, ring(y, 2))
            gf = vgate[:, at].astype(F32)
            uf = vup[:, at].astype(F32)
            sg = jax.nn.sigmoid(gf)
            gate_grad[:, at] = hg * uf * sg * (1.0 + gf * (1.0 - sg))
            up_grad[:, at] = hg * gf * sg
            return 0

        lax.fori_loop(0, FF // 128, cols, 0)
        for cp in out_copies[:2]:
            cp.start()

    def down_part(at, x_):
        k = pl.ds(pl.multiple_of(x_ * 2 * TOK, 2 * TOK), 2 * TOK)
        rows = pl.ds(x_ * 2, 2)
        out = jnp.dot(ht[0, at, k], mb[0, rows].reshape(2 * TOK, DC), preferred_element_type=F32)
        return out + jnp.dot(
            ht[1, at, k], mb[1, rows].reshape(2 * TOK, DC), preferred_element_type=F32
        )

    def down_near():
        def block(i, _):
            at = pl.ds(pl.multiple_of(i * 448, 64), 448)
            near = down_part(at, y) + down_part(at, ring(y, 1)) + down_part(at, ring(y, 3))
            down_grad[at] = near
            return 0

        lax.fori_loop(0, FF // 448, block, 0)

    def down():
        def block(i, _):
            at = pl.ds(pl.multiple_of(i * 448, 64), 448)
            down_grad[at] = down_grad[at] + down_part(at, ring(y, 2))
            return 0

        lax.fori_loop(0, FF // 448, block, 0)
        out_copies[2].start()

    waited = set()

    def once(cp):
        if id(cp) not in waited:
            waited.add(id(cp))
            cp.wait()

    steps = {
        "own": s_own, "far": s_far, "sib": s_sib, "mix": s_mix, "fwd": s_forward,
        "z": s_z, "state": s_state, "ally": s_all_y, "allf": s_all_forward, "map": s_map,
        "tgt": s_target, "tz": s_target_z, "mis": s_mismatch,
        "ey": s_ey, "fy": s_fy, "ef": s_ef, "ff": s_ff, "ee": s_ee, "fe": s_fe,
        "hide": hide, "sta": student_a, "student": student, "stf": student_forward, "stz": student_z, "ste": student_end,
        "hown": hidden_own, "hfar": hidden_far, "hsib": hidden_sib, "hend": hidden_end,
        "turn": turn, "grada": gate_up_near, "downa": down_near, "grads": gate_up, "down": down,
    }
    before = {"mix": l_out, "state": l_resid, "map": l_proj, "mis": l_stud}
    for step in ORDER:
        name, _, q = step.partition(".")
        if name in before:
            once(before[name])
        if q:
            steps[name](int(q))
        else:
            steps[name]()
        while len(started) > IN_FLIGHT:
            started.pop(0).wait_send()
    for cp in started:
        cp.wait_send()
    for cp in out_copies:
        cp.wait()


def hand_out(a, b, c, a_out, b_out, c_out, a_held, b_held, c_held, sem):
    held = (a_held, b_held, c_held)
    ins = [pltpu.make_async_copy(src, v, sem.at[i]) for i, (src, v) in enumerate(zip((a, b, c), held))]
    outs = [
        pltpu.make_async_copy(v, dst, sem.at[3 + i])
        for i, (v, dst) in enumerate(zip(held, (a_out, b_out, c_out)))
    ]
    for cp in ins:
        cp.start()
    for first, then in zip(ins, outs):
        first.wait()
        then.start()
    for cp in outs:
        cp.wait()


def per_device(attn_out, teacher_resid, w_out, projection, student_in, gate_act, up_act, w_down):
    def vmem(*shape, dtype=BF16):
        return pltpu.VMEM(shape, dtype)

    grads = pl.pallas_call(
        kernel,
        out_shape=(
            jax.ShapeDtypeStruct((TOK, FF), F32),
            jax.ShapeDtypeStruct((TOK, FF), F32),
            jax.ShapeDtypeStruct((FF, DC), F32),
        ),
        in_specs=[pl.BlockSpec(memory_space=pl.ANY)] * 8,
        out_specs=(pl.BlockSpec(memory_space=pl.ANY),) * 3,
        scratch_shapes=[
            vmem(TOK, FF, dtype=F32),
            vmem(TOK, FF, dtype=F32),
            vmem(FF, DC, dtype=F32),
            vmem(Q, 4, 2, 2, S, DK),
            vmem(Q, 4, 4, S, DK),
            vmem(Q, 2, 2, S, DK),
            vmem(Q, 2, 4, S, DK),
            vmem(Q, 4, S, DK),
            vmem(Q, 3, S, DK),
            vmem(Q, 4, 4, S, DK),
            vmem(Q, 4, 2, 2, S, DC),
            vmem(Q, 7, 2, S, DC),
            vmem(Q, 2, S, DC, dtype=F32),
            vmem(Q, 2, S, DC),
            vmem(Q, S, DC),
            vmem(TOK, DS),
            vmem(Q, S, DC),
            vmem(2, 8, TOK, DC),
            vmem(TOK, FF),
            vmem(2, FF, 8 * TOK),
            vmem(4, 4, TOK, DC),
            vmem(2, 2, TOK, DC),
            vmem(2, 4, TOK, DC),
            vmem(4, TOK, DC),
            vmem(3, TOK, DC),
            vmem(TOK, DC, dtype=F32),
            vmem(DK, DK),
            vmem(DK, DC),
            vmem(FF, DS),
            vmem(DS, FF),
            vmem(TOK, DK),
            vmem(TOK, DC),
            vmem(TOK, FF),
            vmem(TOK, FF),
            pltpu.SemaphoreType.DMA((N_SLOTS,)),
            pltpu.SemaphoreType.DMA((N_SLOTS,)),
            pltpu.SemaphoreType.DMA((Q + 10,)),
        ],
        compiler_params=pltpu.CompilerParams(
            collective_id=0, has_side_effects=True, vmem_limit_bytes=58 * 2**20
        ),
        name="distill_step",
    )(attn_out, teacher_resid, w_out, projection, student_in, gate_act, up_act, w_down)
    return pl.pallas_call(
        hand_out,
        out_shape=tuple(jax.ShapeDtypeStruct(g.shape, g.dtype) for g in grads),
        in_specs=[pl.BlockSpec(memory_space=pl.ANY)] * 3,
        out_specs=(pl.BlockSpec(memory_space=pl.ANY),) * 3,
        scratch_shapes=[pltpu.VMEM(g.shape, g.dtype) for g in grads] + [pltpu.SemaphoreType.DMA((6,))],
        name="hand_out",
    )(*grads)


def solution(mesh):
    in_specs = (
        P("dp", "tensor"),
        P("tensor", "dp"),
        P("tensor", "dp"),
        P("dp", "tensor"),
        P("dp", "tensor"),
        P("dp", "tensor"),
        P("dp", "tensor"),
        P("tensor", None),
    )
    out_specs = (P("dp", "tensor"), P("dp", "tensor"), P("tensor", "dp"))
    return jax.shard_map(
        per_device, mesh=mesh, in_specs=in_specs, out_specs=out_specs, check_vma=False
    )
```

```python
import functools

import jax
import jax.numpy as jnp
from jax import lax
from jax.experimental import pallas as pl
from jax.experimental.pallas import tpu as pltpu
from jax.sharding import PartitionSpec as P

MESH = pl.DeviceIdType.MESH
F32 = jnp.float32
BF16 = jnp.bfloat16

Q = 4
TOK = 128
S = TOK // Q
DK = 1024
DC = 256
DS = 4096
FF = 896
ORDER = ("own.0", "hide", "sta", "far.0", "own.1", "student", "sib.0", "own.2", "far.1", "own.3", "mix.0", "sib.1", "far.2", "far.3", "hown", "fwd.0", "mix.1", "z.0", "sib.3", "fwd.1", "mix.3", "z.1", "hfar", "sib.2", "state.0", "fwd.3", "mix.2", "state.1", "fwd.2", "z.3", "stf", "ally.0", "z.2", "ally.1", "turn", "state.3", "allf.0", "allf.1", "state.2", "map.1", "hsib", "map.0", "tgt.0", "ally.3", "tgt.1", "stz", "ally.2", "tz.0", "allf.3", "tz.1", "ste", "allf.2", "mis.1", "map.2", "map.3", "tgt.3", "mis.0", "tgt.2", "hend", "ey.1", "fy.1", "ey.0", "tz.3", "fy.0", "ef.1", "tz.2", "ff.1", "mis.3", "ef.0", "ff.0", "fe.1", "mis.2", "ey.3", "fy.3", "ey.2", "fe.0", "fy.2", "ee.1", "ff.3", "ef.3", "ef.2", "ff.2", "grada", "downa", "ee.3", "fe.3", "ee.0", "ee.2", "grads", "fe.2", "down")

A_SLOTS, B_SLOTS, C_SLOTS, D_SLOTS, E_SLOTS = 12, 9, 13, 8, 15
E_GATHER = 4
E_MIRROR = 11
IN_FLIGHT = 60
A0 = 0
B0 = A0 + A_SLOTS * Q
C0 = B0 + B_SLOTS * Q
D0 = C0 + C_SLOTS * Q
E0 = D0 + D_SLOTS * Q
SB0 = E0 + E_SLOTS * Q
H0 = SB0 + B_SLOTS
N_SLOTS = H0 + A_SLOTS


def kernel(
    attn, resid, w_out, proj, stud, gate, up, w_down,
    gate_out, up_out, down_out,
    gate_grad, up_grad, down_grad, g, p1, y1, y2, r, zr, ta, p2, dx, p4, p4b, dz,
    ma, mt, mb, hid, ht, sp, sy1, sy2, sr, szr, so,
    vw_out, vproj, vw_down, vturned, vresid, vstud, vgate, vup,
    ss, rs, ls,
):
    d = lax.axis_index("dp")
    t = lax.axis_index("tensor")
    x, zh, c = d // 4, lax.rem(d // 2, 2), lax.rem(d, 2)
    y, zl = t // 4, lax.rem(t, 4)

    def dev(x_, zh_, c_, y_, zl_):
        return ((x_ * 2 + zh_) * 2 + c_, y_ * 4 + zl_)

    def ring(a, k):
        return lax.rem(a + k, 4)

    sib = dev(x, zh, 1 - c, y, zl)
    far = dev(x, 1 - zh, c, y, zl)
    xs = [dev(ring(x, k), zh, c, y, zl) for k in (1, 2, 3)]
    zs = [dev(x, zh, c, y, ring(zl, k)) for k in (1, 2, 3)]
    yn, yp = dev(x, zh, c, ring(y, 1), zl), dev(x, zh, c, ring(y, 3), zl)
    xo = [dev(ring(x, k), zh, 1 - c, y, zl) for k in (1, 2, 3)]
    mirror_to = [(t, (d // 4) * 4 + k) for k in range(4)]
    mirror_from = [((t // 4) * 4 + k, d) for k in range(4)]
    other = [jnp.logical_or(d != t, lax.rem(d, 4) != k) for k in range(4)]

    def load(i, src, dst):
        return pltpu.make_async_copy(src, dst, ls.at[i])

    own_a = [load(q, attn.at[pl.ds(q * S, S)], g.at[q, x, zh, c]) for q in range(Q)]
    l_gate = load(Q, gate, vgate)
    l_up = load(Q + 1, up, vup)
    l_down = load(Q + 2, w_down, vw_down)
    l_out = load(Q + 3, w_out, vw_out)
    l_proj = load(Q + 4, proj, vproj)
    l_resid = load(Q + 5, resid, vresid)
    l_stud = load(Q + 6, stud, vstud)
    for cp in [l_gate, l_up, l_down, l_out] + own_a + [l_proj, l_resid, l_stud]:
        cp.start()

    out_copies = [
        load(Q + 7, gate_grad, gate_out), load(Q + 8, up_grad, up_out), load(Q + 9, down_grad, down_out),
    ]

    barrier = pltpu.get_barrier_semaphore()
    for peer in [sib, far, yn, yp] + xs + xo + zs:
        pl.semaphore_signal(barrier, 1, device_id=peer, device_id_type=MESH)
    for k in range(4):

        @pl.when(other[k])
        def _():
            pl.semaphore_signal(barrier, 1, device_id=mirror_from[k], device_id_type=MESH)

    pl.semaphore_wait(barrier, jnp.where(d != t, 17, 16))

    started = []

    def send(slot, src, dst, peer):
        cp = pltpu.make_async_remote_copy(
            src, dst, ss.at[slot], rs.at[slot], device_id=peer, device_id_type=MESH
        )
        cp.start()
        started.append(cp)
        return cp

    def gather_dp_own(base, own, place, place2):
        dst = place(x, zh, c)
        m = {}
        m["z"] = send(base, own, dst, far)
        for k in (1, 2, 3):
            m["x", k] = send(base + k, own, dst, xs[k - 1])
        m["s0"] = send(base + 4, own, dst, sib)
        return m

    def gather_dp_far(base, m, place, place2):
        m["z"].wait_recv()
        piece = place(x, 1 - zh, c)
        for k in (1, 2, 3):
            m["zx", k] = send(base + 4 + k, piece, piece, xs[k - 1])
        m["s1"] = send(base + 8, piece, piece, sib)

    def gather_dp_sib(base, m, place, place2):
        for k in (1, 3, 2):
            m["x", k].wait_recv()
            m["zx", k].wait_recv()
            piece = place2(ring(x, 4 - k), c)
            m["s", k] = send(base + 8 + k, piece, piece, sib)

    def gather_dp_end(m):
        m["s0"].wait_recv()
        m["s1"].wait_recv()
        for k in (1, 3, 2):
            m["s", k].wait_recv()

    def scatter_y_first(base, part, a1):
        far_y = ring(y, 2)
        m = {}
        m["h0"] = send(base, part.at[far_y, pl.ds(0, 2)], a1.at[0], yn)
        m["h1"] = send(base + 1, part.at[far_y, pl.ds(2, 2)], a1.at[1], yp)
        return m

    def scatter_y_raw(base, m, part, a2):
        m["r0"] = send(base + 2, part.at[ring(y, 1), pl.ds(2, 2)], a2.at[0, pl.ds(2, 2)], yn)
        m["r1"] = send(base + 3, part.at[ring(y, 3), pl.ds(0, 2)], a2.at[1, pl.ds(0, 2)], yp)

    def scatter_y_forward(base, m, part, a1, a2):
        for side, (lo, to, peer) in enumerate(((0, ring(y, 1), yn), (2, ring(y, 3), yp))):
            m["h%d" % side].wait_recv()
            for i in range(2):
                both = part[to, lo + i].astype(F32) + a1[side, i].astype(F32)
                part[to, lo + i] = both.astype(BF16)
            m["c%d" % side] = send(
                base + 4 + side, part.at[to, pl.ds(lo, 2)], a2.at[side, pl.ds(lo, 2)], peer
            )

    def scatter_z(base, m, part, a2, res, az):
        for n in ("r0", "r1", "c0", "c1"):
            m[n].wait_recv()
        for i in range(4):
            total = part[y, i].astype(F32) + a2[0, i].astype(F32) + a2[1, i].astype(F32)
            res[i] = total.astype(BF16)
        for k in (1, 2, 3):
            m["z", k] = send(base + 5 + k, res.at[ring(zl, k)], az.at[k - 1], zs[k - 1])

    def scatter_end(m, res, az):
        for k in (1, 2, 3):
            m["z", k].wait_recv()
        total = res[zl].astype(F32)
        for k in range(3):
            total += az[k].astype(F32)
        return total

    def gather_z(base, view, early=False):
        own = view(y, zl, 1)
        m = {("z", k): send(base + k - 1, own, own, zs[k - 1]) for k in (1, 2, 3)}
        m["early"] = early
        if early:
            m["y0", 0] = send(base + 3, own, own, yn)
            m["y1", 0] = send(base + 4, own, own, yp)
        return m

    def gather_y(base, m, view):
        if m["early"]:
            for k in (1, 3, 2):
                m["z", k].wait_recv()
                piece = view(y, ring(zl, 4 - k), 1)
                m["y0", k] = send(base + 3 + 2 * k, piece, piece, yn)
                m["y1", k] = send(base + 4 + 2 * k, piece, piece, yp)
        else:
            for k in (1, 2, 3):
                if ("z", k) in m:
                    m["z", k].wait_recv()
            mine = view(y, 0, 4)
            m["y0", 0] = send(base + 3, mine, mine, yn)
            m["y1", 0] = send(base + 4, mine, mine, yp)

    def gather_forward(base, m, view):
        base += 11 if m["early"] else 5
        for side, (far_y, lo, peer) in enumerate(((ring(y, 3), 0, yn), (ring(y, 1), 2, yp))):
            for k in (0, 1, 3, 2) if m["early"] else (0,):
                m["y%d" % side, k].wait_recv()
            half = view(far_y, lo, 2)
            m["f%d" % side] = send(base + side, half, half, peer)

    def gather_end(m):
        m["f0"].wait_recv()
        m["f1"].wait_recv()

    A = [None] * Q
    B = [None] * Q
    C = [None] * Q
    D = [{} for _ in range(Q)]
    E = [None] * Q
    EM = [None] * Q

    def g_place(q):
        return lambda x_, zh_, c_: g.at[q, x_, zh_, c_]

    def g_place2(q):
        return lambda x_, c_: g.at[q, x_, :, c_]

    def ta_view(q):
        return lambda y_, lo, n: ta.at[q, y_, pl.ds(lo, n)]

    def ma_view(q):
        def view(y_, lo, n):
            start = pl.multiple_of((y_ * 4 + lo) * DC, DC)
            return ma.at[pl.ds(q * S, S), pl.ds(start, n * DC)]

        return view

    def mb_view(q):
        rows = pl.ds(q * S, S)

        def view(y_, lo, n):
            if n == 1:
                return mb.at[lax.rem(lo, 2), y_ * 2 + lo // 2, rows]
            if n == 2:
                return mb.at[:, y_ * 2 + lo // 2, rows]
            return mb.at[:, pl.ds(y_ * 2, 2), rows]

        return view

    def mix(q):
        def cols(n, _):
            at = pl.ds(pl.multiple_of(n * 256, 256), 256)
            out = jnp.dot(g[q].reshape(16 * S, DK), vw_out[:, at], preferred_element_type=F32)
            p1[q, :, :, :, at] = out.astype(BF16).reshape(4, 4, S, 256)
            return 0

        lax.fori_loop(0, DK // 256, cols, 0)

    def map_target(q, yg):
        out = jnp.dot(ta[q, yg].reshape(4 * S, DK), vproj[...], preferred_element_type=F32)
        p2[q, yg] = out.astype(BF16).reshape(2, 2, S, DC)

    def s_far(q):
        gather_dp_far(A0 + A_SLOTS * q, A[q], g_place(q), g_place2(q))

    def s_sib(q):
        gather_dp_sib(A0 + A_SLOTS * q, A[q], g_place(q), g_place2(q))

    def s_own(q):
        base = A0 + A_SLOTS * q
        A[q] = gather_dp_own(base, attn.at[pl.ds(q * S, S)], g_place(q), g_place2(q))

    def s_mix(q):
        own_a[q].wait()
        gather_dp_end(A[q])
        mix(q)
        B[q] = scatter_y_first(B0 + B_SLOTS * q, p1.at[q], y1.at[q])
        scatter_y_raw(B0 + B_SLOTS * q, B[q], p1.at[q], y2.at[q])

    def s_forward(q):
        scatter_y_forward(B0 + B_SLOTS * q, B[q], p1.at[q], y1.at[q], y2.at[q])

    def s_z(q):
        scatter_z(B0 + B_SLOTS * q, B[q], p1.at[q], y2.at[q], r.at[q], zr.at[q])

    def s_state(q):
        total = scatter_end(B[q], r.at[q], zr.at[q])
        state = total + vresid[pl.ds(q * S, S)].astype(F32)
        ta[q, y, zl] = state.astype(BF16)
        C[q] = gather_z(C0 + C_SLOTS * q, ta_view(q), early=True)

    def s_all_y(q):
        gather_y(C0 + C_SLOTS * q, C[q], ta_view(q))

    def s_all_forward(q):
        gather_forward(C0 + C_SLOTS * q, C[q], ta_view(q))

    def s_map(q):
        map_target(q, y)
        map_target(q, ring(y, 1))
        map_target(q, ring(y, 3))

    def s_target(q):
        gather_end(C[q])
        map_target(q, ring(y, 2))
        base = D0 + D_SLOTS * q
        for k in (1, 3, 2):
            D[q][k - 1] = send(base + k - 1, p2.at[q, ring(x, k), :, c], dx.at[q, k - 1], xs[k - 1])
            D[q][k + 2] = send(base + k + 2, p2.at[q, ring(x, k), :, 1 - c], dx.at[q, k + 2], xo[k - 1])
        D[q][6] = send(base + 6, p2.at[q, x, :, 1 - c], dx.at[q, 6], sib)

    def s_target_z(q):
        for k in range(7):
            D[q][k].wait_recv()
        total = p2[q, x, :, c].astype(F32)
        for k in range(7):
            total += dx[q, k].astype(F32)
        p4[q] = total
        p4b[q] = total.astype(BF16)
        D[q]["z"] = send(D0 + D_SLOTS * q + 7, p4b.at[q, 1 - zh], dz.at[q], far)

    def s_mismatch(q):
        D[q]["z"].wait_recv()
        rows = pl.ds(q * S, S)
        target = p4[q, zh] + dz[q].astype(F32)
        diff = (vstud[rows].astype(F32) + so[rows] - target).astype(BF16)
        mt[q] = diff
        col = pl.multiple_of(t * DC, DC)
        ma[rows, pl.ds(col, DC)] = diff
        base = E0 + E_SLOTS * q
        for k in range(4):

            @pl.when(other[k])
            def _():
                mirror_copy(q, k, lax.rem(d, 4), d).start()

        @pl.when(d == t)
        def _():
            mb[lax.rem(d, 2), d // 2, rows] = diff

        E[q] = gather_z(base, ma_view(q))

    def mirror_copy(q, k, slot, owner):
        base = E0 + E_SLOTS * q + E_MIRROR
        return pltpu.make_async_remote_copy(
            mt.at[q], mb.at[lax.rem(owner, 2), owner // 2, pl.ds(q * S, S)],
            ss.at[base + k], rs.at[base + slot],
            device_id=mirror_to[k], device_id_type=MESH,
        )

    def s_ey(q):
        gather_y(E0 + E_SLOTS * q, E[q], ma_view(q))

    def s_fy(q):
        for k in range(4):

            @pl.when(other[k])
            def _():
                mirror_copy(q, k, k, (t // 4) * 4 + k).wait_recv()

        EM[q] = {"early": False}
        gather_y(E0 + E_SLOTS * q + E_GATHER, EM[q], mb_view(q))

    def s_ef(q):
        gather_forward(E0 + E_SLOTS * q, E[q], ma_view(q))

    def s_ff(q):
        gather_forward(E0 + E_SLOTS * q + E_GATHER, EM[q], mb_view(q))
        for k in range(4):

            @pl.when(other[k])
            def _():
                mirror_copy(q, k, k, d).wait_send()

    def s_ee(q):
        gather_end(E[q])

    def s_fe(q):
        gather_end(EM[q])

    st = {}

    def ht_place(x_, zh_, c_):
        return ht.at[c_, :, pl.ds(pl.multiple_of((x_ * 2 + zh_) * TOK, TOK), TOK)]

    def ht_place2(x_, c_):
        return ht.at[c_, :, pl.ds(pl.multiple_of(x_ * 2 * TOK, 2 * TOK), 2 * TOK)]

    def hide():
        l_gate.wait()
        l_up.wait()
        gf = vgate[...].astype(F32)
        h = (gf * jax.nn.sigmoid(gf) * vup[...].astype(F32)).astype(BF16)
        hid[...] = h
        ht[c, :, pl.ds(pl.multiple_of((x * 2 + zh) * TOK, TOK), TOK)] = h.astype(F32).T.astype(BF16)

    def student_part(first, last):
        def cols(i, _):
            at = pl.ds(pl.multiple_of(i * DC, DC), DC)
            out = jnp.dot(hid[...], vw_down[:, at], preferred_element_type=F32)
            sp[i // 4, lax.rem(i, 4)] = out.astype(BF16)
            return 0

        lax.fori_loop(first, last, cols, 0)

    def student_a():
        l_down.wait()
        student_part(0, 8)

    def student():
        student_part(8, 16)
        st["m"] = scatter_y_first(SB0, sp, sy1)
        scatter_y_raw(SB0, st["m"], sp, sy2)

    def student_forward():
        scatter_y_forward(SB0, st["m"], sp, sy1, sy2)

    def student_z():
        scatter_z(SB0, st["m"], sp, sy2, sr, szr)

    def student_end():
        so[...] = scatter_end(st["m"], sr, szr)

    def hidden_own():
        st["h"] = gather_dp_own(H0, ht_place(x, zh, c), ht_place, ht_place2)

    def hidden_far():
        gather_dp_far(H0, st["h"], ht_place, ht_place2)

    def hidden_end():
        gather_dp_end(st["h"])

    def hidden_sib():
        gather_dp_sib(H0, st["h"], ht_place, ht_place2)

    def turn():
        def block(i, _):
            at = pl.ds(pl.multiple_of(i * 128, 128), 128)
            vturned[at, :] = vw_down[:, at].T
            return 0

        lax.fori_loop(0, DS // 128, block, 0)

    def hidden_part(at, y_):
        k = pl.ds(pl.multiple_of(y_ * 4 * DC, 4 * DC), 4 * DC)
        return jnp.dot(ma[:, k], vturned[k, at], preferred_element_type=F32)

    def gate_up_near():
        def cols(i, _):
            at = pl.ds(pl.multiple_of(i * 128, 128), 128)
            near = hidden_part(at, y) + hidden_part(at, ring(y, 1)) + hidden_part(at, ring(y, 3))
            gate_grad[:, at] = near
            return 0

        lax.fori_loop(0, FF // 128, cols, 0)

    def gate_up():
        def cols(i, _):
            at = pl.ds(pl.multiple_of(i * 128, 128), 128)
            hg = gate_grad[:, at] + hidden_part(at, ring(y, 2))
            gf = vgate[:, at].astype(F32)
            uf = vup[:, at].astype(F32)
            sg = jax.nn.sigmoid(gf)
            gate_grad[:, at] = hg * uf * sg * (1.0 + gf * (1.0 - sg))
            up_grad[:, at] = hg * gf * sg
            return 0

        lax.fori_loop(0, FF // 128, cols, 0)
        for cp in out_copies[:2]:
            cp.start()

    def down_part(at, x_):
        k = pl.ds(pl.multiple_of(x_ * 2 * TOK, 2 * TOK), 2 * TOK)
        rows = pl.ds(x_ * 2, 2)
        out = jnp.dot(ht[0, at, k], mb[0, rows].reshape(2 * TOK, DC), preferred_element_type=F32)
        return out + jnp.dot(
            ht[1, at, k], mb[1, rows].reshape(2 * TOK, DC), preferred_element_type=F32
        )

    def down_near():
        def block(i, _):
            at = pl.ds(pl.multiple_of(i * 448, 64), 448)
            near = down_part(at, y) + down_part(at, ring(y, 1)) + down_part(at, ring(y, 3))
            down_grad[at] = near
            return 0

        lax.fori_loop(0, FF // 448, block, 0)

    def down():
        def block(i, _):
            at = pl.ds(pl.multiple_of(i * 448, 64), 448)
            down_grad[at] = down_grad[at] + down_part(at, ring(y, 2))
            return 0

        lax.fori_loop(0, FF // 448, block, 0)
        out_copies[2].start()

    waited = set()

    def once(cp):
        if id(cp) not in waited:
            waited.add(id(cp))
            cp.wait()

    steps = {
        "own": s_own, "far": s_far, "sib": s_sib, "mix": s_mix, "fwd": s_forward,
        "z": s_z, "state": s_state, "ally": s_all_y, "allf": s_all_forward, "map": s_map,
        "tgt": s_target, "tz": s_target_z, "mis": s_mismatch,
        "ey": s_ey, "fy": s_fy, "ef": s_ef, "ff": s_ff, "ee": s_ee, "fe": s_fe,
        "hide": hide, "sta": student_a, "student": student, "stf": student_forward, "stz": student_z, "ste": student_end,
        "hown": hidden_own, "hfar": hidden_far, "hsib": hidden_sib, "hend": hidden_end,
        "turn": turn, "grada": gate_up_near, "downa": down_near, "grads": gate_up, "down": down,
    }
    before = {"mix": l_out, "state": l_resid, "map": l_proj, "mis": l_stud}
    for step in ORDER:
        name, _, q = step.partition(".")
        if name in before:
            once(before[name])
        if q:
            steps[name](int(q))
        else:
            steps[name]()
        while len(started) > IN_FLIGHT:
            started.pop(0).wait_send()
    for cp in started:
        cp.wait_send()
    for cp in out_copies:
        cp.wait()


def hand_out(a, b, c, a_out, b_out, c_out, a_held, b_held, c_held, sem):
    held = (a_held, b_held, c_held)
    ins = [pltpu.make_async_copy(src, v, sem.at[i]) for i, (src, v) in enumerate(zip((a, b, c), held))]
    outs = [
        pltpu.make_async_copy(v, dst, sem.at[3 + i])
        for i, (v, dst) in enumerate(zip(held, (a_out, b_out, c_out)))
    ]
    for cp in ins:
        cp.start()
    for first, then in zip(ins, outs):
        first.wait()
        then.start()
    for cp in outs:
        cp.wait()


def per_device(attn_out, teacher_resid, w_out, projection, student_in, gate_act, up_act, w_down):
    def vmem(*shape, dtype=BF16):
        return pltpu.VMEM(shape, dtype)

    grads = pl.pallas_call(
        kernel,
        out_shape=(
            jax.ShapeDtypeStruct((TOK, FF), F32),
            jax.ShapeDtypeStruct((TOK, FF), F32),
            jax.ShapeDtypeStruct((FF, DC), F32),
        ),
        in_specs=[pl.BlockSpec(memory_space=pl.ANY)] * 8,
        out_specs=(pl.BlockSpec(memory_space=pl.ANY),) * 3,
        scratch_shapes=[
            vmem(TOK, FF, dtype=F32),
            vmem(TOK, FF, dtype=F32),
            vmem(FF, DC, dtype=F32),
            vmem(Q, 4, 2, 2, S, DK),
            vmem(Q, 4, 4, S, DK),
            vmem(Q, 2, 2, S, DK),
            vmem(Q, 2, 4, S, DK),
            vmem(Q, 4, S, DK),
            vmem(Q, 3, S, DK),
            vmem(Q, 4, 4, S, DK),
            vmem(Q, 4, 2, 2, S, DC),
            vmem(Q, 7, 2, S, DC),
            vmem(Q, 2, S, DC, dtype=F32),
            vmem(Q, 2, S, DC),
            vmem(Q, S, DC),
            vmem(TOK, DS),
            vmem(Q, S, DC),
            vmem(2, 8, TOK, DC),
            vmem(TOK, FF),
            vmem(2, FF, 8 * TOK),
            vmem(4, 4, TOK, DC),
            vmem(2, 2, TOK, DC),
            vmem(2, 4, TOK, DC),
            vmem(4, TOK, DC),
            vmem(3, TOK, DC),
            vmem(TOK, DC, dtype=F32),
            vmem(DK, DK),
            vmem(DK, DC),
            vmem(FF, DS),
            vmem(DS, FF),
            vmem(TOK, DK),
            vmem(TOK, DC),
            vmem(TOK, FF),
            vmem(TOK, FF),
            pltpu.SemaphoreType.DMA((N_SLOTS,)),
            pltpu.SemaphoreType.DMA((N_SLOTS,)),
            pltpu.SemaphoreType.DMA((Q + 10,)),
        ],
        compiler_params=pltpu.CompilerParams(
            collective_id=0, has_side_effects=True, vmem_limit_bytes=58 * 2**20
        ),
        name="distill_step",
    )(attn_out, teacher_resid, w_out, projection, student_in, gate_act, up_act, w_down)
    return pl.pallas_call(
        hand_out,
        out_shape=tuple(jax.ShapeDtypeStruct(g.shape, g.dtype) for g in grads),
        in_specs=[pl.BlockSpec(memory_space=pl.ANY)] * 3,
        out_specs=(pl.BlockSpec(memory_space=pl.ANY),) * 3,
        scratch_shapes=[pltpu.VMEM(g.shape, g.dtype) for g in grads] + [pltpu.SemaphoreType.DMA((6,))],
        name="hand_out",
    )(*grads)


def solution(mesh):
    in_specs = (
        P("dp", "tensor"),
        P("tensor", "dp"),
        P("tensor", "dp"),
        P("dp", "tensor"),
        P("dp", "tensor"),
        P("dp", "tensor"),
        P("dp", "tensor"),
        P("tensor", None),
    )
    out_specs = (P("dp", "tensor"), P("dp", "tensor"), P("tensor", "dp"))
    return jax.shard_map(
        per_device, mesh=mesh, in_specs=in_specs, out_specs=out_specs, check_vma=False
    )
```
